512 devices in a mesh: grp: 32 (over x, z), harm: 16 (over y, core).
Axes of the slice: x: 4, y: 8, z: 8, core: 2. Of those that a mesh axis runs over, the one named last changes fastest.
Arguments:
- initial_coef: float32 [64, 16384], P('harm', 'grp'), may hold values from -4 to 4
- load_coef: float32 [64, 16384], P('harm', 'grp'), may hold values from -24 to 24
- mass: float32 [16384], P('grp'), may hold values from 0.5 to 2
- stiffness: float32 [128, 3, 128, 128], P('grp'), may hold values from -0.012 to 12, as said below
- block_offset: int32 [128, 2], P('grp'), may hold values from -2 to 2, as said below
- joint_dofs: int32 [32, 512], P('grp'), may hold values from 0 to 511, each once within a row
- joint_owner: int32 [32, 256], P('grp'), may hold values from 0 to 31, as said below
- elem_stiff: float32 [32, 16, 768], P('grp'), may hold values from 0.03 to 0.3
- slip_force: float32 [32, 16, 768], P('grp'), may hold values from 0.05 to 1
Outputs:
- solution: float32 [64, 16384], P('harm', 'grp')
- residual: float32 [64, 16384], P('harm', 'grp')
The draws below stay inside these ranges and needn't reach their ends.
Inputs may be any that keep to these rules, and one draw needn't show every extreme that they name: Each diagonal entry of a block stiffness[i, 0] lies between 8 and 12, every other entry between -0.012 and 0.012. `block_offset`: column 0 is -1 or -2, column 1 is 1 or 2. `joint_dofs`: each row is a permutation of 0 to 511. `joint_owner`: among the joints of one row at most 24 have the same owner, and one owner has exactly 24 joints of every row.
All inputs are finite; a program needn't handle non-finite values.
Results may differ from the reference program's by a relative error of at most 0.0003.
Values sent between devices are 32-bit elements; how exact they have to be, the bound alone decides.
A program may use at most 64 MiB of HBM per device.

```python
import math
import jax
import jax.numpy as jnp
from jax import lax

BS = 128
HARM = 32
NE = 16
NEWTON = 2
NCOEF = 64
NT = 128
DOF_DEV = 512
NDOF = 16384
NB = 128
JOINT_DEV = 256
CAP = 24
SLOTS = 768
N_GRP = 32


def draw_stiffness(key, part):
    first_key, second_key = jax.random.split(key)
    coupling = jax.random.uniform(first_key, (NB, 3, BS, BS), jnp.float32, -0.012, 0.012)
    diagonal = jax.random.uniform(second_key, (NB, BS), jnp.float32, 8.0, 12.0)
    identity = jnp.arange(BS)[:, None] == jnp.arange(BS)[None, :]
    own_block = jnp.where(identity[None, :, :], diagonal[:, :, None], coupling[:, 0])
    return coupling.at[:, 0].set(own_block)


def draw_block_offset(key, part):
    reach = jax.random.randint(key, (NB, 2), 0, 2, dtype=jnp.int32)
    direction = jnp.where(jnp.arange(2, dtype=jnp.int32) == 0, -1, 1).astype(jnp.int32)
    return (direction[None, :] * (1 + reach)).astype(jnp.int32)


def draw_joint_owner(key, part):
    heavy_key, order_key, turn_key = jax.random.split(key, 3)
    heavy = jax.random.randint(heavy_key, (), 0, N_GRP, dtype=jnp.int32)
    row_keys = jax.random.split(order_key, N_GRP)
    ranks = jax.vmap(lambda row_key: jax.random.permutation(row_key, JOINT_DEV))(row_keys).astype(jnp.int32)
    rotation = jax.random.randint(turn_key, (N_GRP, 1), 0, N_GRP - 1, dtype=jnp.int32)
    others = (heavy + 1 + (ranks - CAP + rotation) % (N_GRP - 1)) % N_GRP
    return jnp.where(ranks < CAP, heavy, others).astype(jnp.int32)


def level_of(rng, shape, cuts, low, high):
    def one(axis_at, blocks):
        steps = jax.random.uniform(jax.random.fold_in(jax.random.fold_in(rng, 6), axis_at), (blocks,), jnp.float32, low / len(cuts), high / len(cuts))
        return jnp.repeat(jnp.exp(steps), shape[axis_at] // blocks).reshape((-1,) + (1,) * (len(shape) - axis_at - 1))

    loudness = one(*cuts[0])
    for cut in cuts[1:]:
        loudness = loudness * one(*cut)
    return loudness


def normal_values(stream_key, dims, scale, most, cuts=(), kind=jnp.bfloat16):
    entries = jax.random.normal(stream_key, dims, jnp.float32) * scale
    if len(cuts) > 0:
        entries = level_of(stream_key, dims, cuts, -0.22, 0.18) * entries
    return jnp.clip(entries, min=-most, max=most).astype(kind)


def setup_inputs(seed: int = 0) -> dict:
    seeds = jax.random.split(jax.random.key(seed), 10)
    initial_coef = normal_values(seeds[0], (NCOEF, NDOF), 0.5, 4.0, ((0, 16), (1, 32)), jnp.float32)
    load_coef = normal_values(seeds[1], (NCOEF, NDOF), 4.0, 24.0, ((0, 16), (1, 32)), jnp.float32)
    mass = jnp.clip(jnp.exp(math.log(2.0) - 1.3862944 * jax.random.uniform(seeds[2], (NDOF,), jnp.float32) ** level_of(seeds[2], (NDOF,), ((0, 32),), -0.2, 0.2)), 0.5, 2.0)
    stiffness = draw_stiffness(jax.random.fold_in(seeds[9], 71), 0)
    block_offset = draw_block_offset(jax.random.fold_in(seeds[9], 71), 0)
    joint_dofs = jax.vmap(lambda own: jax.random.permutation(own, DOF_DEV))(jax.random.split(seeds[5], N_GRP)).reshape((N_GRP, DOF_DEV)).astype(jnp.int32)
    joint_owner = draw_joint_owner(jax.random.fold_in(seeds[9], 71), 0)
    elem_stiff = jnp.clip(jnp.exp(math.log(0.3) - 2.3025852 * jax.random.uniform(seeds[7], (N_GRP, NE, SLOTS), jnp.float32) ** level_of(seeds[7], (N_GRP, NE, SLOTS), ((0, 32),), -0.2, 0.2)), 0.03, 0.3)
    slip_force = jnp.clip(jnp.exp(math.log(1.0) - 2.9957323 * jax.random.uniform(seeds[8], (N_GRP, NE, SLOTS), jnp.float32) ** level_of(seeds[8], (N_GRP, NE, SLOTS), ((0, 32),), -0.2, 0.2)), 0.05, 1.0)
    return {"initial_coef": initial_coef, "load_coef": load_coef, "mass": mass, "stiffness": stiffness, "block_offset": block_offset, "joint_dofs": joint_dofs, "joint_owner": joint_owner, "elem_stiff": elem_stiff, "slip_force": slip_force}


highest = lax.Precision.HIGHEST
omega_base = 0.03125


def harmonic_of(coefs, harmonics):
    return jnp.where(coefs <= harmonics, coefs, coefs - harmonics)


def fourier_basis(times, coefs, harmonics, samples):
    freq = harmonic_of(coefs, harmonics)
    phase = (times[:, None] * freq[None, :]) % samples
    angle = phase.astype(jnp.float32) * (2.0 * math.pi / samples)
    return jnp.where((coefs > harmonics)[None, :], jnp.sin(angle), jnp.cos(angle))


def coef_weights(coefs, samples):
    return jnp.where(coefs == 0, 1.0 / samples, 2.0 / samples).astype(jnp.float32)


def reference(initial_coef, load_coef, mass, stiffness, block_offset, joint_dofs, joint_owner, elem_stiff, slip_force):
    coefs = jnp.arange(NCOEF, dtype=jnp.int32)
    times = jnp.arange(NT, dtype=jnp.int32)
    synth = fourier_basis(times, coefs, HARM, NT)
    analysis = (synth * coef_weights(coefs, NT)[None, :]).T
    freq = harmonic_of(coefs, HARM).astype(jnp.float32) * omega_base
    dynamic = (freq * freq)[:, None] * mass[None, :]
    kdiag = jnp.diagonal(stiffness[:, 0], axis1=1, axis2=2).reshape(NDOF)
    precond = 1.0 / (kdiag[None, :] - dynamic)

    sources = jnp.arange(N_GRP, dtype=jnp.int32)
    onehot = (joint_owner[:, :, None] == sources[None, None, :]).astype(jnp.int32)
    rank = jnp.sum((jnp.cumsum(onehot, axis=1) - onehot) * onehot, axis=2)
    column = sources[:, None] * CAP + rank
    joint_count = N_GRP * JOINT_DEV
    k_joint = elem_stiff[joint_owner, :, column].reshape(joint_count, NE).T
    s_joint = slip_force[joint_owner, :, column].reshape(joint_count, NE).T
    base = (sources * DOF_DEV)[:, None]
    side_a = (base + joint_dofs[:, :JOINT_DEV]).reshape(joint_count)
    side_b = (base + joint_dofs[:, JOINT_DEV:]).reshape(joint_count)

    offsets = jnp.concatenate([jnp.zeros((NB, 1), jnp.int32), block_offset.astype(jnp.int32)], axis=1)
    block_index = jnp.arange(NB, dtype=jnp.int32)[:, None] + 2 + offsets

    def apply_stiffness(coef_field):
        blocks = coef_field.reshape(NCOEF, NB, BS)
        padded = jnp.pad(blocks, ((0, 0), (2, 2), (0, 0)))
        taken = padded[:, block_index, :]
        product = jnp.einsum("ikrs,ciks->cir", stiffness, taken, precision=highest)
        return product.reshape(NCOEF, NDOF)

    def joint_forces(relative):
        movement = relative - jnp.roll(relative, 1, axis=0)

        def advance(force, move_row):
            force = jnp.clip(force + k_joint * move_row[None, :], -s_joint, s_joint)
            return force, jnp.sum(force, axis=0)

        _, totals = lax.scan(advance, jnp.zeros((NE, joint_count), jnp.float32), movement)
        return totals

    def residual_of(coef_field):
        disp_time = jnp.dot(synth, coef_field, precision=highest)
        relative = disp_time[:, side_a] - disp_time[:, side_b]
        totals = joint_forces(relative)
        force_time = jnp.zeros((NT, NDOF), jnp.float32).at[:, side_a].add(totals).at[:, side_b].add(-totals)
        nonlinear = jnp.dot(analysis, force_time, precision=highest)
        return apply_stiffness(coef_field) - dynamic * coef_field + nonlinear - load_coef

    current = initial_coef
    latest = load_coef
    for step in range(NEWTON):
        latest = residual_of(current)
        current = current - precond * latest
    return current, latest
```

```python
import math

import jax
import jax.numpy as jnp
import numpy as np
from jax import lax
from jax.experimental import pallas as pl
from jax.experimental.pallas import tpu as pltpu
from jax.sharding import PartitionSpec as P

HARM = 32
NT = 128
GRP = 32
PARTS = 16
CHIPS = 8
CD = 4
DOF = 512
JOINTS = 256
CAP = 24
NE = 16
f32, bf16, i32 = jnp.float32, jnp.bfloat16, jnp.int32
MESH = pl.DeviceIdType.MESH


def basis_tables():
    row = np.arange(PARTS * 8)
    coef = 4 * (row // 8) + row % 4
    harmonic = np.where(coef <= HARM, coef, coef - HARM)
    angle = 2.0 * math.pi * ((np.arange(NT)[:, None] * harmonic[None, :]) % NT) / NT
    synth = np.where(coef > HARM, np.sin(angle), np.cos(angle))
    move = (synth - np.roll(synth, 1, axis=0)) * np.where(row % 8 < 4, 1.0, -1.0)
    project = (synth * np.where(coef == 0, 1.0, 2.0) / NT).T

    def split(x):
        x = x.astype(np.float32)
        high = x.astype(jnp.bfloat16)
        return [high, (x - high.astype(np.float32)).astype(jnp.bfloat16)]

    return np.stack(split(move) + split(project))


def split2(x):
    high = x.astype(bf16).astype(f32)
    return high, x - high


def terms2(x):
    return jnp.concatenate(split2(x), axis=0).astype(bf16)


def terms3(x):
    high, rest = split2(x)
    mid, low = split2(rest)
    return jnp.concatenate([high, mid, low], axis=0).astype(bf16)


def mm(a, b):
    return lax.dot_general(a, b, (((1,), (0,)), ((), ())), preferred_element_type=f32)


def mm_t(a, b):
    return lax.dot_general(a, b, (((1,), (1,)), ((), ())), preferred_element_type=f32)


def select3(x, weights, product):
    n = x.shape[0]
    y = product(terms3(x), weights)
    return y[:n] + y[n : 2 * n] + y[2 * n :]


def kernel(
    u_hbm,
    load_hbm,
    mass_hbm,
    offset_hbm,
    dofs_hbm,
    owner_hbm,
    basis_hbm,
    stiff_hbm,
    k_hbm,
    s_hbm,
    out_u,
    out_r,
    u_v,
    load_v,
    mass_v,
    offset_v,
    dofs_v,
    owner_v,
    basis_v,
    stiff_v,
    table_v,
    near_hi,
    near_lo,
    far_hi,
    far_lo,
    perm,
    slots,
    send1,
    recv1,
    send2,
    recv2,
    sendp,
    recvp,
    move_v,
    total_v,
    sendg,
    recvg,
    current,
    halo,
    local_sem,
    send_sem,
    recv_sem,
    halo_send,
    halo_recv,
):
    g = lax.axis_index("grp")
    h = lax.axis_index("harm")
    chip = lax.div(h, 2)
    core = lax.rem(h, 2)
    right = lax.rem(g + 1, GRP)
    left = lax.rem(g + GRP - 1, GRP)

    fetches = [
        pltpu.make_async_copy(src, dst, local_sem.at[i])
        for i, (src, dst) in enumerate(
            [
                (owner_hbm, owner_v),
                (dofs_hbm, dofs_v),
                (u_hbm, u_v),
                (load_hbm, load_v),
                (mass_hbm, mass_v),
                (offset_hbm, offset_v),
                (k_hbm, table_v.at[0]),
                (s_hbm, table_v.at[1]),
                (stiff_hbm, stiff_v),
                (basis_hbm, basis_v),
            ]
        )
    ]
    for fetch in fetches:
        fetch.start()

    barrier = pltpu.get_barrier_semaphore()
    for k in range(1, PARTS):
        pl.semaphore_signal(
            barrier, inc=1, device_id=(g, lax.rem(h + k, PARTS)), device_id_type=MESH
        )
    for side in (left, right):
        pl.semaphore_signal(barrier, inc=1, device_id=(side, h), device_id_type=MESH)
    source_part = lax.rem(lax.div(g, 2) + PARTS - 2, PARTS)
    for k in range(4):
        pl.semaphore_signal(
            barrier, inc=1, device_id=(4 * chip + k, source_part), device_id_type=MESH
        )

    fetches[0].wait()
    fetches[1].wait()
    owner = owner_v[...]
    own = jnp.where(lax.broadcasted_iota(i32, (GRP, JOINTS), 0) == owner, 1.0, 0.0)
    before = jnp.where(
        lax.broadcasted_iota(i32, (JOINTS, JOINTS), 0)
        < lax.broadcasted_iota(i32, (JOINTS, JOINTS), 1),
        1.0,
        0.0,
    )
    earlier = mm(own.astype(bf16), before.astype(bf16))
    rank = jnp.sum(earlier * own, axis=0, keepdims=True).astype(i32)
    slot = (owner >> 2) * 128 + (owner & 3) * CAP + rank
    row = lax.broadcasted_iota(i32, (128, JOINTS), 0)
    for m in range(CHIPS):
        slots[m * 128 : (m + 1) * 128, :] = jnp.where(row == slot - m * 128, 1.0, 0.0).astype(bf16)
    dofs = dofs_v[...]
    row = lax.broadcasted_iota(i32, (128, DOF), 0)
    for m in range(DOF // 128):
        perm[m * 128 : (m + 1) * 128, :] = jnp.where(row == dofs - m * 128, 1.0, 0.0).astype(bf16)

    fetches[6].wait()
    fetches[7].wait()
    target = 2 * lax.rem(h + 2, PARTS)
    lane = lax.broadcasted_iota(i32, (NE, 128), 1)
    first = lax.rem(g, 4) * CAP
    wanted = (lane >= first) & (lane < first + CAP)
    for t in range(2):
        column = (target + t) * CAP
        tile = jnp.minimum(lax.div(column, 128), 4)
        shift = lax.rem(first - (column - tile * 128) + 512, 256)
        for a in range(2):
            part = table_v[a, 0, :, pl.ds(pl.multiple_of(tile * 128, 128), 256)]
            rolled = pltpu.roll(part, shift, 1)[:, :128]
            sendp[t, a * NE : (a + 1) * NE, :] = jnp.where(wanted, rolled, 0.0)

    fetches[8].wait()
    eye = lax.broadcasted_iota(i32, (128, 128), 0) == lax.broadcasted_iota(i32, (128, 128), 1)
    diagonals = []

    def store(hi, lo, i, at, block):
        high, low = split2(block)
        hi[i, :, at : at + 128] = high.astype(bf16)
        lo[i, :, at : at + 128] = low.astype(bf16)

    for i in range(4):
        own_block = stiff_v[i, 0]
        diagonals.append(jnp.sum(jnp.where(eye, own_block, 0.0), axis=0, keepdims=True))
        store(near_hi, near_lo, i, 0, jnp.where(eye, 0.0, own_block))
        store(near_hi, near_lo, i, 128, stiff_v[i, 2 if i < 2 else 1])
        store(far_hi, far_lo, i, 0, stiff_v[i, 1 if i < 2 else 2])
    kdiag = jnp.concatenate(diagonals, axis=1)
    coef = 4 * h + lax.broadcasted_iota(i32, (CD, DOF), 0)
    freq = jnp.where(coef <= HARM, coef, coef - HARM).astype(f32) * (1.0 / HARM)
    fetches[4].wait()
    net = kdiag - (freq * freq) * mass_v[...]
    precond = 1.0 / net

    fetches[2].wait()
    u0 = u_v[...]
    upper = lax.broadcasted_iota(i32, (8, 128), 0) < CD

    def to_slots(x, sign, out):
        pairs = select3(x, perm[...], mm)
        relative = pairs[:, :JOINTS] + sign * pairs[:, JOINTS:]
        by_slot = select3(relative, slots[...], mm_t)
        for m in range(CHIPS):
            out[m] = by_slot[:, m * 128 : (m + 1) * 128]

    sign = jnp.where(lax.broadcasted_iota(i32, (8, JOINTS), 0) < CD, -1.0, 1.0)
    to_slots(jnp.concatenate([u0, precond], axis=0), sign, send1)

    pl.semaphore_wait(barrier, PARTS - 1 + 2 + 4)

    def send_halo(n, ref):
        copies = [
            pltpu.make_async_remote_copy(
                src_ref=ref.at[:, 256:512] if k == 0 else ref.at[:, 0:256],
                dst_ref=halo.at[n, k],
                send_sem=halo_send.at[n, k],
                recv_sem=halo_recv.at[n, k],
                device_id=(side, h),
                device_id_type=MESH,
            )
            for k, side in enumerate((right, left))
        ]
        for copy in copies:
            copy.start()
        return copies

    halo0 = send_halo(0, u_v)

    def send_parts(n, src, dst):
        for k in range(1, PARTS):
            to = lax.rem(h + k, PARTS)
            pltpu.make_async_remote_copy(
                src_ref=src.at[lax.div(to, 2)],
                dst_ref=dst.at[h],
                send_sem=send_sem.at[n],
                recv_sem=recv_sem.at[n],
                device_id=(g, to),
                device_id_type=MESH,
            ).start()
        dst[h] = src[chip]

    def settle(ref, sem):
        pltpu.make_async_copy(ref, ref, sem).wait()

    send_parts(0, send1, recv1)
    for t in range(2):
        for c in range(2):
            pltpu.make_async_remote_copy(
                src_ref=sendp.at[t],
                dst_ref=recvp.at[lax.rem(g, 4)],
                send_sem=send_sem.at[2],
                recv_sem=recv_sem.at[2],
                device_id=(target + t, 2 * lax.div(g, 4) + c),
                device_id_type=MESH,
            ).start()

    fetches[5].wait()
    offset = offset_v[...]

    def block(u, i):
        return u[:, i * 128 : (i + 1) * 128]

    def nearer(i, k):
        return jnp.abs(offset[i : i + 1, k : k + 1]) == 1

    def apply(lhs, hi, lo):
        terms = terms2(lhs)
        a = mm_t(terms, hi)
        b = mm_t(terms, lo)
        return a[:CD] + (a[CD:] + b[:CD])

    def near_product(u):
        parts = []
        for i in range(4):
            if i < 2:
                other = jnp.where(nearer(i, 1), block(u, i + 1), block(u, i + 2))
            else:
                other = jnp.where(nearer(i, 0), block(u, i - 1), block(u, i - 2))
            lhs = jnp.concatenate([block(u, i), other], axis=1)
            parts.append(apply(lhs, near_hi[i], near_lo[i]))
        return jnp.concatenate(parts, axis=1)

    def far_product(u, n):
        low = jnp.where(g > 0, halo[n, 0], 0.0)
        high = jnp.where(g < GRP - 1, halo[n, 1], 0.0)
        others = [
            jnp.where(nearer(0, 0), block(low, 1), block(low, 0)),
            jnp.where(nearer(1, 0), block(u, 0), block(low, 1)),
            jnp.where(nearer(2, 1), block(u, 3), block(high, 0)),
            jnp.where(nearer(3, 1), block(high, 0), block(high, 1)),
        ]
        return jnp.concatenate(
            [apply(others[i], far_hi[i], far_lo[i]) for i in range(4)], axis=1
        )

    fetches[3].wait()
    load = load_v[...]
    part = load - near_product(u0)
    for copy in halo0:
        copy.wait_recv()
    base = precond * (part - far_product(u0, 0))
    to_slots(jnp.concatenate([base, jnp.zeros_like(base)], axis=0), -1.0, send2)
    send_parts(1, send2, recv2)

    fetches[9].wait()
    settle(recv1.at[pl.ds(0, PARTS - 1)], recv_sem.at[0])
    settle(recvp, recv_sem.at[2])
    table = recvp[0] + recvp[1] + recvp[2] + recvp[3]
    k_slot = table[:NE]
    s_slot = table[NE:]

    def forces(x, n):
        high, low = split2(x)
        high, low = high.astype(bf16), low.astype(bf16)
        move_v[...] = mm(basis_v[0], high) + (mm(basis_v[1], high) + mm(basis_v[0], low))

        def samples(i, force):
            at = pl.multiple_of(8 * i, 8)
            move = move_v[pl.ds(at, 8), :]
            sums = []
            for j in range(8):
                force = jnp.clip(force + k_slot * move[j : j + 1, :], -s_slot, s_slot)
                sums.append(jnp.sum(force, axis=0, keepdims=True))
            total_v[pl.ds(at, 8), :] = jnp.concatenate(sums, axis=0)
            return force

        lax.fori_loop(0, NT // 8, samples, jnp.zeros((NE, 128), f32))
        high, low = split2(total_v[...])
        high, low = high.astype(bf16), low.astype(bf16)
        coefs = mm(basis_v[2], high) + (mm(basis_v[3], high) + mm(basis_v[2], low))
        sendg[n] = coefs.reshape(PARTS, 8, 128)
        for k in range(1, CHIPS):
            to = lax.rem(chip + k, CHIPS) * 2 + core
            pltpu.make_async_remote_copy(
                src_ref=sendg.at[n, to],
                dst_ref=recvg.at[n, chip],
                send_sem=send_sem.at[3 + n],
                recv_sem=recv_sem.at[3 + n],
                device_id=(g, to),
                device_id_type=MESH,
            ).start()
        recvg[n, chip] = sendg[n, h]

    def nonlinear(n):
        settle(recvg.at[n, pl.ds(0, CHIPS - 1)], recv_sem.at[3 + n])
        lanes = jnp.concatenate([recvg[n, m][:CD] for m in range(CHIPS)], axis=1)
        joint = select3(lanes, slots[...], mm)
        return select3(jnp.concatenate([joint, -joint], axis=1), perm[...], mm_t)

    first_part = upper[None]
    forces(jnp.where(first_part, recv1[...], 0.0).reshape(PARTS * 8, 128), 0)
    settle(recv2.at[pl.ds(0, PARTS - 1)], recv_sem.at[1])
    forces(jnp.where(first_part, recv2[...], recv1[...] * sendg[0]).reshape(PARTS * 8, 128), 1)

    u1 = base - precond * nonlinear(0)
    current[...] = u1
    halo1 = send_halo(1, current)
    part = near_product(u1) + net * u1 - load
    for copy in halo1:
        copy.wait_recv()
    part = part + far_product(u1, 1)
    residual = part + nonlinear(1)
    out_r[...] = residual
    out_u[...] = u1 - precond * residual

    for copy in halo0 + halo1:
        copy.wait_send()
    settle(recv1.at[pl.ds(0, PARTS - 1)], send_sem.at[0])
    settle(recv2.at[pl.ds(0, PARTS - 1)], send_sem.at[1])
    settle(recvp, send_sem.at[2])
    for n in range(2):
        settle(recvg.at[n, pl.ds(0, CHIPS - 1)], send_sem.at[3 + n])


def local(u, load, mass, stiffness, offset, dofs, owner, k_table, s_table):
    basis = jnp.asarray(basis_tables())
    hbm = pl.BlockSpec(memory_space=pltpu.HBM)
    vmem = pl.BlockSpec(memory_space=pltpu.VMEM)
    return pl.pallas_call(
        kernel,
        out_shape=[jax.ShapeDtypeStruct((CD, DOF), f32)] * 2,
        in_specs=[hbm] * 10,
        out_specs=[vmem] * 2,
        scratch_shapes=[
            pltpu.VMEM((CD, DOF), f32),
            pltpu.VMEM((CD, DOF), f32),
            pltpu.VMEM((1, DOF), f32),
            pltpu.VMEM((4, 2), i32),
            pltpu.VMEM((1, DOF), i32),
            pltpu.VMEM((1, JOINTS), i32),
            pltpu.VMEM((4, 128, 128), bf16),
            pltpu.VMEM((4, 3, 128, 128), f32),
            pltpu.VMEM((2, 1, NE, GRP * CAP), f32),
            pltpu.VMEM((4, 128, 256), bf16),
            pltpu.VMEM((4, 128, 256), bf16),
            pltpu.VMEM((4, 128, 128), bf16),
            pltpu.VMEM((4, 128, 128), bf16),
            pltpu.VMEM((DOF, DOF), bf16),
            pltpu.VMEM((CHIPS * 128, JOINTS), bf16),
            pltpu.VMEM((CHIPS, 8, 128), f32),
            pltpu.VMEM((PARTS, 8, 128), f32),
            pltpu.VMEM((CHIPS, 8, 128), f32),
            pltpu.VMEM((PARTS, 8, 128), f32),
            pltpu.VMEM((2, 2 * NE, 128), f32),
            pltpu.VMEM((4, 2 * NE, 128), f32),
            pltpu.VMEM((NT, 128), f32),
            pltpu.VMEM((NT, 128), f32),
            pltpu.VMEM((2, PARTS, 8, 128), f32),
            pltpu.VMEM((2, CHIPS, 8, 128), f32),
            pltpu.VMEM((CD, DOF), f32),
            pltpu.VMEM((2, 2, CD, 256), f32),
            pltpu.SemaphoreType.DMA((10,)),
            pltpu.SemaphoreType.DMA((5,)),
            pltpu.SemaphoreType.DMA((5,)),
            pltpu.SemaphoreType.DMA((2, 2)),
            pltpu.SemaphoreType.DMA((2, 2)),
        ],
        compiler_params=pltpu.CompilerParams(
            collective_id=0, has_side_effects=True, vmem_limit_bytes=16 * 2**20
        ),
    )(u, load, mass.reshape(1, DOF), offset, dofs, owner, basis, stiffness, k_table, s_table)


def solution(mesh):
    in_specs = (
        P("harm", "grp"),
        P("harm", "grp"),
        P("grp"),
        P("grp", None, None, None),
        P("grp", None),
        P("grp", None),
        P("grp", None),
        P("grp", None, None),
        P("grp", None, None),
    )
    out_specs = (P("harm", "grp"), P("harm", "grp"))

    def run(*args):
        return tuple(local(*args))

    return jax.shard_map(run, mesh=mesh, in_specs=in_specs, out_specs=out_specs, check_vma=False)
```

```python
import math

import jax
import jax.numpy as jnp
import numpy as np
from jax import lax
from jax.experimental import pallas as pl
from jax.experimental.pallas import tpu as pltpu
from jax.sharding import PartitionSpec as P

HARM = 32
NT = 128
GRP = 32
PARTS = 16
CHIPS = 8
CD = 4
DOF = 512
JOINTS = 256
CAP = 24
NE = 16
f32, bf16, i32 = jnp.float32, jnp.bfloat16, jnp.int32
MESH = pl.DeviceIdType.MESH


def basis_tables():
    row = np.arange(PARTS * 8)
    coef = 4 * (row // 8) + row % 4
    harmonic = np.where(coef <= HARM, coef, coef - HARM)
    angle = 2.0 * math.pi * ((np.arange(NT)[:, None] * harmonic[None, :]) % NT) / NT
    synth = np.where(coef > HARM, np.sin(angle), np.cos(angle))
    move = (synth - np.roll(synth, 1, axis=0)) * np.where(row % 8 < 4, 1.0, -1.0)
    project = (synth * np.where(coef == 0, 1.0, 2.0) / NT).T

    def split(x):
        x = x.astype(np.float32)
        high = x.astype(jnp.bfloat16)
        return [high, (x - high.astype(np.float32)).astype(jnp.bfloat16)]

    short = np.zeros((NT, 128))
    short[:, : PARTS * CD] = move[:, row % 8 < 4]
    return np.stack(split(move) + split(project) + split(short))


def split2(x):
    high = x.astype(bf16).astype(f32)
    return high, x - high


def terms2(x):
    return jnp.concatenate(split2(x), axis=0).astype(bf16)


def terms3(x):
    high, rest = split2(x)
    mid, low = split2(rest)
    return jnp.concatenate([high, mid, low], axis=0).astype(bf16)


def mm(a, b):
    return lax.dot_general(a, b, (((1,), (0,)), ((), ())), preferred_element_type=f32)


def mm_t(a, b):
    return lax.dot_general(a, b, (((1,), (1,)), ((), ())), preferred_element_type=f32)


def select3(x, weights, product):
    n = x.shape[0]
    y = product(terms3(x), weights)
    return y[:n] + y[n : 2 * n] + y[2 * n :]


def kernel(
    u_hbm,
    load_hbm,
    mass_hbm,
    offset_hbm,
    dofs_hbm,
    owner_hbm,
    basis_hbm,
    stiff_hbm,
    k_hbm,
    s_hbm,
    out_u,
    out_r,
    u_v,
    load_v,
    mass_v,
    offset_v,
    dofs_v,
    owner_v,
    basis_v,
    stiff_v,
    table_v,
    near_hi,
    near_lo,
    far_hi,
    far_lo,
    perm,
    slots,
    slots_side,
    send1,
    recv1,
    send2,
    recv2,
    sendp,
    recvp,
    move_v,
    total_v,
    sendg,
    recvg,
    recvg_side,
    fixed,
    fixed_side,
    base_v,
    base_side,
    u_side,
    local_sem,
    send_sem,
    recv_sem,
    side_send,
    side_recv,
):
    g = lax.axis_index("grp")
    h = lax.axis_index("harm")
    chip = lax.div(h, 2)
    core = lax.rem(h, 2)
    sides = (lax.rem(g + 1, GRP), lax.rem(g + GRP - 1, GRP))

    barrier = pltpu.get_barrier_semaphore()

    def greet(group, part):
        pl.semaphore_signal(barrier, inc=1, device_id=(group, part), device_id_type=MESH)

    source = 4 * lax.rem(chip + GRP - g, CHIPS)
    for k in range(4):
        greet(source + k, 2 * chip + 1 - core)
    for k in (4, 3, 5, 2, 6, 1, 7, 0):
        part = 2 * lax.rem(chip + k, CHIPS)
        for side in sides:
            greet(side, part + core)
        if k > 0:
            greet(g, part + core)
        greet(g, part + 1 - core)

    fetches = [
        pltpu.make_async_copy(src, dst, local_sem.at[i])
        for i, (src, dst) in enumerate(
            [
                (owner_hbm, owner_v),
                (dofs_hbm, dofs_v),
                (u_hbm, u_v),
                (load_hbm, load_v),
                (mass_hbm, mass_v),
                (offset_hbm, offset_v),
                (k_hbm, table_v.at[0]),
                (s_hbm, table_v.at[1]),
                (stiff_hbm, stiff_v),
                (basis_hbm, basis_v),
            ]
        )
    ]
    for fetch in fetches:
        fetch.start()

    fetches[0].wait()
    fetches[1].wait()
    owner = owner_v[...]
    own = jnp.where(lax.broadcasted_iota(i32, (GRP, JOINTS), 0) == owner, 1.0, 0.0)
    before = jnp.where(
        lax.broadcasted_iota(i32, (JOINTS, JOINTS), 0)
        < lax.broadcasted_iota(i32, (JOINTS, JOINTS), 1),
        1.0,
        0.0,
    )
    earlier = mm(own.astype(bf16), before.astype(bf16))
    rank = jnp.sum(earlier * own, axis=0, keepdims=True)
    tile = (((owner >> 2) + g) & 7).astype(f32)
    lane = ((owner & 3) * CAP).astype(f32) + rank
    ones = jnp.ones((1, JOINTS), f32)
    dofs = dofs_v[...]
    row = lax.broadcasted_iota(i32, (128, DOF), 0)
    for m in range(DOF // 128):
        perm[m * 128 : (m + 1) * 128, :] = jnp.where(row == dofs - m * 128, 1.0, 0.0).astype(bf16)
    by_joint = jnp.concatenate(
        [
            jnp.concatenate([tile, lane, ones], axis=0),
            jnp.concatenate([tile, lane, -ones], axis=0),
        ],
        axis=1,
    )
    by_dof = mm_t(by_joint.astype(bf16), perm[...])
    slot_f = by_dof[0:1] * 128.0 + by_dof[1:2]
    slot = slot_f.astype(i32)
    sign = by_dof[2:3]
    for m in range(CHIPS):
        slots[m * 128 : (m + 1) * 128, :] = jnp.where(row == slot - m * 128, 1.0, 0.0).astype(bf16)

    fetches[2].wait()
    u0 = u_v[...]

    def to_slots(x, out):
        by_slot = select3(x, slots[...], mm_t)
        for m in range(CHIPS):
            out[m] = by_slot[:, m * 128 : (m + 1) * 128]

    to_slots(u0 * sign, send1)

    fetches[6].wait()
    fetches[7].wait()
    target = lax.rem(chip + CHIPS - lax.div(g, 4), CHIPS)
    at = lax.broadcasted_iota(i32, (NE, 128), 1)
    first = lax.rem(g, 4) * CAP
    wanted = (at >= first) & (at < first + CAP)
    for t in range(4):
        column = (target + 8 * t) * CAP
        begin = jnp.minimum(lax.div(column, 128), 4)
        shift = lax.rem(first - (column - begin * 128) + 512, 256)
        for a in range(2):
            part = table_v[a, 0, :, pl.ds(pl.multiple_of(begin * 128, 128), 256)]
            rolled = pltpu.roll(part, shift, 1)[:, :128]
            sendp[t, a * NE : (a + 1) * NE, :] = jnp.where(wanted, rolled, 0.0)

    pl.semaphore_wait(barrier, PARTS - 1 + 2 * CHIPS + 4)

    def send_sides(n, src, dst):
        copies = [
            pltpu.make_async_remote_copy(
                src_ref=src.at[:, 256:512] if k == 0 else src.at[:, 0:256],
                dst_ref=dst.at[k],
                send_sem=side_send.at[n, k],
                recv_sem=side_recv.at[n, k],
                device_id=(side, h),
                device_id_type=MESH,
            )
            for k, side in enumerate(sides)
        ]
        for copy in copies:
            copy.start()
        return copies

    def send_parts(n, src, dst):
        for k in (8, 7, 9, 6, 10, 5, 11, 4, 12, 3, 13, 2, 14, 1, 15):
            to = lax.rem(h + k, PARTS)
            pltpu.make_async_remote_copy(
                src_ref=src.at[lax.div(to, 2)],
                dst_ref=dst.at[h],
                send_sem=send_sem.at[n],
                recv_sem=recv_sem.at[n],
                device_id=(g, to),
                device_id_type=MESH,
            ).start()
        dst[h] = src[chip]

    def settle(ref, sem):
        pltpu.make_async_copy(ref, ref, sem).wait()

    halo0 = send_sides(0, u_v, u_side)
    for t in range(4):
        pltpu.make_async_remote_copy(
            src_ref=sendp.at[t],
            dst_ref=recvp.at[lax.rem(g, 4)],
            send_sem=send_sem.at[2],
            recv_sem=recv_sem.at[2],
            device_id=(target + 8 * t, 2 * chip + 1 - core),
            device_id_type=MESH,
        ).start()
    send_parts(0, send1, recv1)

    fetches[8].wait()
    eye = lax.broadcasted_iota(i32, (128, 128), 0) == lax.broadcasted_iota(i32, (128, 128), 1)
    diagonals = []

    def store(hi, lo, i, at, block):
        high, low = split2(block)
        hi[i, :, at : at + 128] = high.astype(bf16)
        lo[i, :, at : at + 128] = low.astype(bf16)

    for i in range(4):
        own_block = stiff_v[i, 0]
        diagonals.append(jnp.sum(jnp.where(eye, own_block, 0.0), axis=0, keepdims=True))
        store(near_hi, near_lo, i, 0, jnp.where(eye, 0.0, own_block))
        store(near_hi, near_lo, i, 128, stiff_v[i, 2 if i < 2 else 1])
        store(far_hi, far_lo, i, 0, stiff_v[i, 1 if i < 2 else 2])
    kdiag = jnp.concatenate(diagonals, axis=1)
    coef = 4 * h + lax.broadcasted_iota(i32, (CD, DOF), 0)
    freq = jnp.where(coef <= HARM, coef, coef - HARM).astype(f32) * (1.0 / HARM)
    fetches[4].wait()
    net = kdiag - (freq * freq) * mass_v[...]
    precond = 1.0 / net
    signed = precond * sign
    fixed[...] = jnp.concatenate([signed, jnp.broadcast_to(slot_f, (CD, DOF))], axis=0)
    halof = send_sides(1, fixed, fixed_side)

    fetches[5].wait()
    offset = offset_v[...]

    def block(u, i):
        return u[:, i * 128 : (i + 1) * 128]

    def nearer(i, k):
        return jnp.abs(offset[k : k + 1, i : i + 1]) == 1

    def apply(lhs, hi, lo):
        terms = terms2(lhs)
        a = mm_t(terms, hi)
        b = mm_t(terms, lo)
        return a[:CD] + (a[CD:] + b[:CD])

    def near_product(u):
        parts = []
        for i in range(4):
            if i < 2:
                other = jnp.where(nearer(i, 1), block(u, i + 1), block(u, i + 2))
            else:
                other = jnp.where(nearer(i, 0), block(u, i - 1), block(u, i - 2))
            lhs = jnp.concatenate([block(u, i), other], axis=1)
            parts.append(apply(lhs, near_hi[i], near_lo[i]))
        return jnp.concatenate(parts, axis=1)

    def far_product(u, low, high):
        low = jnp.where(g > 0, low, 0.0)
        high = jnp.where(g < GRP - 1, high, 0.0)
        others = [
            jnp.where(nearer(0, 0), block(low, 1), block(low, 0)),
            jnp.where(nearer(1, 0), block(u, 0), block(low, 1)),
            jnp.where(nearer(2, 1), block(u, 3), block(high, 0)),
            jnp.where(nearer(3, 1), block(high, 0), block(high, 1)),
        ]
        return jnp.concatenate(
            [apply(others[i], far_hi[i], far_lo[i]) for i in range(4)], axis=1
        )

    fetches[3].wait()
    load = load_v[...]
    part = load - near_product(u0)
    for copy in halo0:
        copy.wait_recv()
    base = precond * (part - far_product(u0, u_side[0], u_side[1]))
    to_slots(jnp.concatenate([base * sign, precond], axis=0), send2)
    send_parts(1, send2, recv2)
    base_v[...] = base
    halob = send_sides(2, base_v, base_side)

    for copy in halof:
        copy.wait_recv()
    row = lax.broadcasted_iota(i32, (128, DOF // 2), 0)
    for k in range(2):
        slot_side = fixed_side[k, CD : CD + 1, :].astype(i32)
        for m in range(CHIPS):
            slots_side[k, m * 128 : (m + 1) * 128, :] = jnp.where(
                row == slot_side - m * 128, 1.0, 0.0
            ).astype(bf16)

    fetches[9].wait()
    settle(recv1.at[pl.ds(0, PARTS - 1)], recv_sem.at[0])
    settle(recvp, recv_sem.at[2])
    table = recvp[0] + recvp[1] + recvp[2] + recvp[3]
    k_slot = table[:NE]
    s_slot = table[NE:]

    def forces(x, n, high_t, low_t):
        high, low = split2(x)
        high, low = high.astype(bf16), low.astype(bf16)
        move_v[...] = mm(high_t, high) + (mm(low_t, high) + mm(high_t, low))

        def samples(i, force):
            at = pl.multiple_of(8 * i, 8)
            move = move_v[pl.ds(at, 8), :]
            sums = []
            for j in range(8):
                force = jnp.clip(force + k_slot * move[j : j + 1, :], -s_slot, s_slot)
                sums.append(jnp.sum(force, axis=0, keepdims=True))
            total_v[pl.ds(at, 8), :] = jnp.concatenate(sums, axis=0)
            return force

        lax.fori_loop(0, NT // 8, samples, jnp.zeros((NE, 128), f32))
        high, low = split2(total_v[...])
        high, low = high.astype(bf16), low.astype(bf16)
        coefs = mm(basis_v[2], high) + (mm(basis_v[3], high) + mm(basis_v[2], low))
        sendg[n] = coefs.reshape(PARTS, 8, 128)
        for k in (4, 3, 5, 2, 6, 1, 7, 0):
            to = 2 * lax.rem(chip + k, CHIPS) + core
            if n == 0:
                for d, side in enumerate(sides):
                    pltpu.make_async_remote_copy(
                        src_ref=sendg.at[0, to],
                        dst_ref=recvg_side.at[d, chip],
                        send_sem=send_sem.at[5],
                        recv_sem=recv_sem.at[5],
                        device_id=(side, to),
                        device_id_type=MESH,
                    ).start()
            if k > 0:
                pltpu.make_async_remote_copy(
                    src_ref=sendg.at[n, to],
                    dst_ref=recvg.at[n, chip],
                    send_sem=send_sem.at[3 + n],
                    recv_sem=recv_sem.at[3 + n],
                    device_id=(g, to),
                    device_id_type=MESH,
                ).start()
        recvg[n, chip] = sendg[n, h]

    def to_dofs(x, weights):
        lanes = jnp.concatenate([x[m][:CD] for m in range(CHIPS)], axis=1)
        return select3(lanes, weights, mm)

    upper = lax.broadcasted_iota(i32, (1, 8, 128), 1) < CD
    forces(recv1[...].reshape(PARTS * CD, 128), 0, basis_v[4, :, : PARTS * CD], basis_v[5, :, : PARTS * CD])
    settle(recv2.at[pl.ds(0, PARTS - 1)], recv_sem.at[1])
    forces(
        (recv2[...] * jnp.where(upper, 1.0, sendg[0])).reshape(PARTS * 8, 128),
        1,
        basis_v[0],
        basis_v[1],
    )

    settle(recvg.at[0, pl.ds(0, CHIPS - 1)], recv_sem.at[3])
    u1 = base - signed * to_dofs(recvg[0], slots[...])
    part = near_product(u1) + net * u1 - load
    for copy in halob:
        copy.wait_recv()
    settle(recvg_side, recv_sem.at[5])
    low, high = [
        base_side[k] - fixed_side[k, :CD, :] * to_dofs(recvg_side[k], slots_side[k])
        for k in range(2)
    ]
    part = part + far_product(u1, low, high)
    settle(recvg.at[1, pl.ds(0, CHIPS - 1)], recv_sem.at[4])
    residual = part + sign * to_dofs(recvg[1], slots[...])
    out_r[...] = residual
    out_u[...] = u1 - precond * residual

    for copy in halo0 + halof + halob:
        copy.wait_send()
    settle(recv1.at[pl.ds(0, PARTS - 1)], send_sem.at[0])
    settle(recv2.at[pl.ds(0, PARTS - 1)], send_sem.at[1])
    settle(recvp, send_sem.at[2])
    for n in range(2):
        settle(recvg.at[n, pl.ds(0, CHIPS - 1)], send_sem.at[3 + n])
    settle(recvg_side, send_sem.at[5])


def local(u, load, mass, stiffness, offset, dofs, owner, k_table, s_table):
    basis = jnp.asarray(basis_tables())
    hbm = pl.BlockSpec(memory_space=pltpu.HBM)
    vmem = pl.BlockSpec(memory_space=pltpu.VMEM)
    return pl.pallas_call(
        kernel,
        out_shape=[jax.ShapeDtypeStruct((CD, DOF), f32)] * 2,
        in_specs=[hbm] * 10,
        out_specs=[vmem] * 2,
        scratch_shapes=[
            pltpu.VMEM((CD, DOF), f32),
            pltpu.VMEM((CD, DOF), f32),
            pltpu.VMEM((1, DOF), f32),
            pltpu.VMEM((2, 4), i32),
            pltpu.VMEM((1, DOF), i32),
            pltpu.VMEM((1, JOINTS), i32),
            pltpu.VMEM((6, 128, 128), bf16),
            pltpu.VMEM((4, 3, 128, 128), f32),
            pltpu.VMEM((2, 1, NE, GRP * CAP), f32),
            pltpu.VMEM((4, 128, 256), bf16),
            pltpu.VMEM((4, 128, 256), bf16),
            pltpu.VMEM((4, 128, 128), bf16),
            pltpu.VMEM((4, 128, 128), bf16),
            pltpu.VMEM((DOF, DOF), bf16),
            pltpu.VMEM((CHIPS * 128, DOF), bf16),
            pltpu.VMEM((2, CHIPS * 128, DOF // 2), bf16),
            pltpu.VMEM((CHIPS, CD, 128), f32),
            pltpu.VMEM((PARTS, CD, 128), f32),
            pltpu.VMEM((CHIPS, 8, 128), f32),
            pltpu.VMEM((PARTS, 8, 128), f32),
            pltpu.VMEM((4, 2 * NE, 128), f32),
            pltpu.VMEM((4, 2 * NE, 128), f32),
            pltpu.VMEM((NT, 128), f32),
            pltpu.VMEM((NT, 128), f32),
            pltpu.VMEM((2, PARTS, 8, 128), f32),
            pltpu.VMEM((2, CHIPS, 8, 128), f32),
            pltpu.VMEM((2, CHIPS, 8, 128), f32),
            pltpu.VMEM((8, DOF), f32),
            pltpu.VMEM((2, 8, DOF // 2), f32),
            pltpu.VMEM((CD, DOF), f32),
            pltpu.VMEM((2, CD, DOF // 2), f32),
            pltpu.VMEM((2, CD, DOF // 2), f32),
            pltpu.SemaphoreType.DMA((10,)),
            pltpu.SemaphoreType.DMA((6,)),
            pltpu.SemaphoreType.DMA((6,)),
            pltpu.SemaphoreType.DMA((3, 2)),
            pltpu.SemaphoreType.DMA((3, 2)),
        ],
        compiler_params=pltpu.CompilerParams(
            collective_id=0, has_side_effects=True, vmem_limit_bytes=60 * 2**20
        ),
    )(u, load, mass.reshape(1, DOF), offset.T, dofs, owner, basis, stiffness, k_table, s_table)


def solution(mesh):
    in_specs = (
        P("harm", "grp"),
        P("harm", "grp"),
        P("grp"),
        P("grp", None, None, None),
        P("grp", None),
        P("grp", None),
        P("grp", None),
        P("grp", None, None),
        P("grp", None, None),
    )
    out_specs = (P("harm", "grp"), P("harm", "grp"))

    def run(*args):
        return tuple(local(*args))

    return jax.shard_map(run, mesh=mesh, in_specs=in_specs, out_specs=out_specs, check_vma=False)
```

```python
import math

import jax
import jax.numpy as jnp
import numpy as np
from jax import lax
from jax.experimental import pallas as pl
from jax.experimental.pallas import tpu as pltpu
from jax.sharding import PartitionSpec as P

HARM = 32
NT = 128
GRP = 32
PARTS = 16
CHIPS = 8
CD = 4
DOF = 512
JOINTS = 256
CAP = 24
NE = 16
f32, bf16, i32 = jnp.float32, jnp.bfloat16, jnp.int32
MESH = pl.DeviceIdType.MESH


def basis_tables():
    row = np.arange(PARTS * 8)
    coef = 4 * (row // 8) + row % 4
    harmonic = np.where(coef <= HARM, coef, coef - HARM)
    angle = 2.0 * math.pi * ((np.arange(NT)[:, None] * harmonic[None, :]) % NT) / NT
    synth = np.where(coef > HARM, np.sin(angle), np.cos(angle))
    move = (synth - np.roll(synth, 1, axis=0)) * np.where(row % 8 < 4, 1.0, -1.0)
    project = (synth * np.where(coef == 0, 1.0, 2.0) / NT).T

    def split(x):
        x = x.astype(np.float32)
        high = x.astype(jnp.bfloat16)
        return [high, (x - high.astype(np.float32)).astype(jnp.bfloat16)]

    short = np.zeros((NT, 128))
    short[:, : PARTS * CD] = move[:, row % 8 < 4]
    return np.stack(split(move) + split(project) + split(short))


def split2(x):
    high = x.astype(bf16).astype(f32)
    return high, x - high


def terms2(x):
    return jnp.concatenate(split2(x), axis=0).astype(bf16)


def terms3(x):
    high, rest = split2(x)
    mid, low = split2(rest)
    return jnp.concatenate([high, mid, low], axis=0).astype(bf16)


def mm(a, b):
    return lax.dot_general(a, b, (((1,), (0,)), ((), ())), preferred_element_type=f32)


def mm_t(a, b):
    return lax.dot_general(a, b, (((1,), (1,)), ((), ())), preferred_element_type=f32)


def select3(x, weights, product):
    n = x.shape[0]
    y = product(terms3(x), weights)
    return y[:n] + y[n : 2 * n] + y[2 * n :]


def kernel(
    u_hbm,
    load_hbm,
    mass_hbm,
    offset_hbm,
    dofs_hbm,
    owner_hbm,
    basis_hbm,
    stiff_hbm,
    k_hbm,
    s_hbm,
    out,
    u_v,
    load_v,
    mass_v,
    offset_v,
    dofs_v,
    owner_v,
    basis_v,
    stiff_v,
    table_v,
    near_hi,
    near_lo,
    far_hi,
    far_lo,
    perm,
    slots,
    slots_side,
    send1,
    recv1,
    send2,
    recv2,
    sendp,
    recvp,
    move_v,
    total_v,
    sendg,
    recvg,
    recvg_side,
    fixed,
    fixed_side,
    base_v,
    base_side,
    u_side,
    local_sem,
    send_sem,
    recv_sem,
    side_send,
    side_recv,
):
    g = lax.axis_index("grp")
    h = lax.axis_index("harm")
    chip = lax.div(h, 2)
    core = lax.rem(h, 2)
    sides = (lax.rem(g + 1, GRP), lax.rem(g + GRP - 1, GRP))

    barrier = pltpu.get_barrier_semaphore()

    def greet(group, part):
        pl.semaphore_signal(barrier, inc=1, device_id=(group, part), device_id_type=MESH)

    source = 4 * lax.rem(chip + GRP - g, CHIPS)
    for k in range(4):
        greet(source + k, 2 * chip + 1 - core)
    for k in (4, 3, 5, 2, 6, 1, 7, 0):
        part = 2 * lax.rem(chip + k, CHIPS)
        for side in sides:
            greet(side, part + core)
        if k > 0:
            greet(g, part + core)
        greet(g, part + 1 - core)

    fetches = [
        pltpu.make_async_copy(src, dst, local_sem.at[i])
        for i, (src, dst) in enumerate(
            [
                (owner_hbm, owner_v),
                (dofs_hbm, dofs_v),
                (u_hbm, u_v),
                (load_hbm, load_v),
                (mass_hbm, mass_v),
                (offset_hbm, offset_v),
                (k_hbm, table_v.at[0]),
                (s_hbm, table_v.at[1]),
                (stiff_hbm, stiff_v),
                (basis_hbm, basis_v),
            ]
        )
    ]
    for fetch in fetches:
        fetch.start()

    fetches[0].wait()
    fetches[1].wait()
    owner = owner_v[...]
    own = jnp.where(lax.broadcasted_iota(i32, (GRP, JOINTS), 0) == owner, 1.0, 0.0)
    before = jnp.where(
        lax.broadcasted_iota(i32, (JOINTS, JOINTS), 0)
        < lax.broadcasted_iota(i32, (JOINTS, JOINTS), 1),
        1.0,
        0.0,
    )
    earlier = mm(own.astype(bf16), before.astype(bf16))
    rank = jnp.sum(earlier * own, axis=0, keepdims=True)
    tile = (((owner >> 2) + g) & 7).astype(f32)
    lane = ((owner & 3) * CAP).astype(f32) + rank
    ones = jnp.ones((1, JOINTS), f32)
    dofs = dofs_v[...]
    row = lax.broadcasted_iota(i32, (128, DOF), 0)
    for m in range(DOF // 128):
        perm[m * 128 : (m + 1) * 128, :] = jnp.where(row == dofs - m * 128, 1.0, 0.0).astype(bf16)
    by_joint = jnp.concatenate(
        [
            jnp.concatenate([tile, lane, ones], axis=0),
            jnp.concatenate([tile, lane, -ones], axis=0),
        ],
        axis=1,
    )
    by_dof = mm_t(by_joint.astype(bf16), perm[...])
    slot_f = by_dof[0:1] * 128.0 + by_dof[1:2]
    slot = slot_f.astype(i32)
    sign = by_dof[2:3]
    for m in range(CHIPS):
        slots[m * 128 : (m + 1) * 128, :] = jnp.where(row == slot - m * 128, 1.0, 0.0).astype(bf16)

    fetches[2].wait()
    u0 = u_v[...]

    def to_slots(x, out):
        by_slot = select3(x, slots[...], mm_t)
        for m in range(CHIPS):
            out[m] = by_slot[:, m * 128 : (m + 1) * 128]

    to_slots(u0 * sign, send1)

    fetches[6].wait()
    fetches[7].wait()
    target = lax.rem(chip + CHIPS - lax.div(g, 4), CHIPS)
    at = lax.broadcasted_iota(i32, (8, 128), 1)
    quarters = [(at >= q * CAP) & (at < (q + 1) * CAP) for q in range(4)]
    for t in range(4):
        column = (target + 8 * t) * CAP
        begin = jnp.minimum(lax.div(column, 128), 4)
        packed = jnp.zeros((8, 128), f32)
        for q in range(4):
            rows = pl.ds(8 * (q % 2), 8)
            part = table_v[q // 2, 0, rows, pl.ds(pl.multiple_of(begin * 128, 128), 256)]
            shift = lax.rem(q * CAP - (column - begin * 128) + 512, 256)
            packed = jnp.where(quarters[q], pltpu.roll(part, shift, 1)[:, :128], packed)
        sendp[t] = packed

    fetches[8].wait()
    eye = lax.broadcasted_iota(i32, (128, 128), 0) == lax.broadcasted_iota(i32, (128, 128), 1)
    diagonals = []

    def store(hi, lo, i, at, block):
        high, low = split2(block)
        hi[i, :, at : at + 128] = high.astype(bf16)
        lo[i, :, at : at + 128] = low.astype(bf16)

    for i in range(4):
        own_block = stiff_v[i, 0]
        diagonals.append(jnp.sum(jnp.where(eye, own_block, 0.0), axis=0, keepdims=True))
        store(near_hi, near_lo, i, 0, jnp.where(eye, 0.0, own_block))
        store(near_hi, near_lo, i, 128, stiff_v[i, 2 if i < 2 else 1])
        store(far_hi, far_lo, i, 0, stiff_v[i, 1 if i < 2 else 2])
    kdiag = jnp.concatenate(diagonals, axis=1)
    coef = 4 * h + lax.broadcasted_iota(i32, (CD, DOF), 0)
    freq = jnp.where(coef <= HARM, coef, coef - HARM).astype(f32) * (1.0 / HARM)
    fetches[4].wait()
    net = kdiag - (freq * freq) * mass_v[...]
    precond = 1.0 / net
    signed = precond * sign
    fixed[...] = jnp.concatenate([signed, jnp.broadcast_to(slot_f, (CD, DOF))], axis=0)
    fetches[5].wait()
    offset = offset_v[...]

    def block(u, i):
        return u[:, i * 128 : (i + 1) * 128]

    def nearer(i, k):
        return jnp.abs(offset[k : k + 1, i : i + 1]) == 1

    def apply(lhs, hi, lo):
        terms = terms2(lhs)
        a = mm_t(terms, hi)
        b = mm_t(terms, lo)
        return a[:CD] + (a[CD:] + b[:CD])

    def near_product(u):
        parts = []
        for i in range(4):
            if i < 2:
                other = jnp.where(nearer(i, 1), block(u, i + 1), block(u, i + 2))
            else:
                other = jnp.where(nearer(i, 0), block(u, i - 1), block(u, i - 2))
            lhs = jnp.concatenate([block(u, i), other], axis=1)
            parts.append(apply(lhs, near_hi[i], near_lo[i]))
        return jnp.concatenate(parts, axis=1)

    def far_product(u, low, high):
        low = jnp.where(g > 0, low, 0.0)
        high = jnp.where(g < GRP - 1, high, 0.0)
        others = [
            jnp.where(nearer(0, 0), block(low, 1), block(low, 0)),
            jnp.where(nearer(1, 0), block(u, 0), block(low, 1)),
            jnp.where(nearer(2, 1), block(u, 3), block(high, 0)),
            jnp.where(nearer(3, 1), block(high, 0), block(high, 1)),
        ]
        return jnp.concatenate(
            [apply(others[i], far_hi[i], far_lo[i]) for i in range(4)], axis=1
        )

    fetches[3].wait()
    load = load_v[...]
    part = load - near_product(u0)
    pl.semaphore_wait(barrier, PARTS - 1 + 2 * CHIPS + 4)

    def send_sides(n, src, dst):
        copies = [
            pltpu.make_async_remote_copy(
                src_ref=src.at[:, 256:512] if k == 0 else src.at[:, 0:256],
                dst_ref=dst.at[k],
                send_sem=side_send.at[n, k],
                recv_sem=side_recv.at[n, k],
                device_id=(side, h),
                device_id_type=MESH,
            )
            for k, side in enumerate(sides)
        ]
        for copy in copies:
            copy.start()
        return copies

    def send_parts(n, src, dst):
        for k in (8, 7, 9, 6, 10, 5, 11, 4, 12, 3, 13, 2, 14, 1, 15):
            to = lax.rem(h + k, PARTS)
            pltpu.make_async_remote_copy(
                src_ref=src.at[lax.div(to, 2)],
                dst_ref=dst.at[h],
                send_sem=send_sem.at[n],
                recv_sem=recv_sem.at[n],
                device_id=(g, to),
                device_id_type=MESH,
            ).start()
        dst[h] = src[chip]

    def settle(ref, sem):
        pltpu.make_async_copy(ref, ref, sem).wait()

    halo0 = send_sides(0, u_v, u_side)
    halof = send_sides(1, fixed, fixed_side)
    for t in range(4):
        pltpu.make_async_remote_copy(
            src_ref=sendp.at[t],
            dst_ref=recvp.at[lax.rem(g, 4)],
            send_sem=send_sem.at[2],
            recv_sem=recv_sem.at[2],
            device_id=(target + 8 * t, 2 * chip + 1 - core),
            device_id_type=MESH,
        ).start()
    send_parts(0, send1, recv1)


    for copy in halo0:
        copy.wait_recv()
    base = precond * (part - far_product(u0, u_side[0], u_side[1]))
    to_slots(jnp.concatenate([base * sign, precond], axis=0), send2)
    send_parts(1, send2, recv2)
    base_v[...] = base
    halob = send_sides(2, base_v, base_side)

    for copy in halof:
        copy.wait_recv()
    row = lax.broadcasted_iota(i32, (128, DOF // 2), 0)
    for k in range(2):
        slot_side = fixed_side[k, CD : CD + 1, :].astype(i32)
        for m in range(CHIPS):
            slots_side[k, m * 128 : (m + 1) * 128, :] = jnp.where(
                row == slot_side - m * 128, 1.0, 0.0
            ).astype(bf16)

    fetches[9].wait()
    settle(recv1.at[pl.ds(0, PARTS - 1)], recv_sem.at[0])
    settle(recvp, recv_sem.at[2])
    table = []
    for r in range(4):
        rows = jnp.zeros((8, 128), f32)
        for q in range(4):
            part = recvp[q]
            if q != r:
                part = pltpu.roll(part, ((q - r) * CAP) % 128, 1)
            rows = jnp.where(quarters[q], part, rows)
        table.append(rows)
    k_slot = jnp.concatenate(table[:2], axis=0)
    s_slot = jnp.concatenate(table[2:], axis=0)

    def forces(x, n, high_t, low_t):
        high, low = split2(x)
        high, low = high.astype(bf16), low.astype(bf16)
        move_v[...] = mm(high_t, high) + (mm(low_t, high) + mm(high_t, low))

        def samples(i, force):
            at = pl.multiple_of(8 * i, 8)
            move = move_v[pl.ds(at, 8), :]
            sums = []
            for j in range(8):
                force = jnp.clip(force + k_slot * move[j : j + 1, :], -s_slot, s_slot)
                sums.append(jnp.sum(force, axis=0, keepdims=True))
            total_v[pl.ds(at, 8), :] = jnp.concatenate(sums, axis=0)
            return force

        lax.fori_loop(0, NT // 8, samples, jnp.zeros((NE, 128), f32))
        high, low = split2(total_v[...])
        high, low = high.astype(bf16), low.astype(bf16)
        coefs = mm(basis_v[2], high) + (mm(basis_v[3], high) + mm(basis_v[2], low))
        sendg[n] = coefs.reshape(PARTS, 8, 128)
        for k in (4, 3, 5, 2, 6, 1, 7, 0):
            to = 2 * lax.rem(chip + k, CHIPS) + core
            if n == 0:
                for d, side in enumerate(sides):
                    pltpu.make_async_remote_copy(
                        src_ref=sendg.at[0, to],
                        dst_ref=recvg_side.at[d, chip],
                        send_sem=send_sem.at[5],
                        recv_sem=recv_sem.at[5],
                        device_id=(side, to),
                        device_id_type=MESH,
                    ).start()
            if k > 0:
                pltpu.make_async_remote_copy(
                    src_ref=sendg.at[n, to],
                    dst_ref=recvg.at[n, chip],
                    send_sem=send_sem.at[3 + n],
                    recv_sem=recv_sem.at[3 + n],
                    device_id=(g, to),
                    device_id_type=MESH,
                ).start()
        recvg[n, chip] = sendg[n, h]

    def to_dofs(x, weights):
        lanes = jnp.concatenate([x[m][:CD] for m in range(CHIPS)], axis=1)
        return select3(lanes, weights, mm)

    upper = lax.broadcasted_iota(i32, (1, 8, 128), 1) < CD
    forces(recv1[...].reshape(PARTS * CD, 128), 0, basis_v[4, :, : PARTS * CD], basis_v[5, :, : PARTS * CD])
    settle(recv2.at[pl.ds(0, PARTS - 1)], recv_sem.at[1])
    forces(
        (recv2[...] * jnp.where(upper, 1.0, sendg[0])).reshape(PARTS * 8, 128),
        1,
        basis_v[0],
        basis_v[1],
    )

    settle(recvg.at[0, pl.ds(0, CHIPS - 1)], recv_sem.at[3])
    u1 = base - signed * to_dofs(recvg[0], slots[...])
    part = near_product(u1) + net * u1 - load
    for copy in halob:
        copy.wait_recv()
    settle(recvg_side, recv_sem.at[5])
    low, high = [
        base_side[k] - fixed_side[k, :CD, :] * to_dofs(recvg_side[k], slots_side[k])
        for k in range(2)
    ]
    part = part + far_product(u1, low, high)
    settle(recvg.at[1, pl.ds(0, CHIPS - 1)], recv_sem.at[4])
    residual = part + sign * to_dofs(recvg[1], slots[...])
    out[1] = residual
    out[0] = u1 - precond * residual

    for copy in halo0 + halof + halob:
        copy.wait_send()
    settle(recv1.at[pl.ds(0, PARTS - 1)], send_sem.at[0])
    settle(recv2.at[pl.ds(0, PARTS - 1)], send_sem.at[1])
    settle(recvp, send_sem.at[2])
    for n in range(2):
        settle(recvg.at[n, pl.ds(0, CHIPS - 1)], send_sem.at[3 + n])
    settle(recvg_side, send_sem.at[5])


def local(u, load, mass, stiffness, offset, dofs, owner, k_table, s_table):
    basis = jnp.asarray(basis_tables())
    hbm = pl.BlockSpec(memory_space=pltpu.HBM)
    vmem = pl.BlockSpec(memory_space=pltpu.VMEM)
    out = pl.pallas_call(
        kernel,
        out_shape=pltpu.VMEM((2, CD, DOF), f32),
        in_specs=[hbm] * 10,
        out_specs=vmem,
        scratch_shapes=[
            pltpu.VMEM((CD, DOF), f32),
            pltpu.VMEM((CD, DOF), f32),
            pltpu.VMEM((1, DOF), f32),
            pltpu.VMEM((2, 4), i32),
            pltpu.VMEM((1, DOF), i32),
            pltpu.VMEM((1, JOINTS), i32),
            pltpu.VMEM((6, 128, 128), bf16),
            pltpu.VMEM((4, 3, 128, 128), f32),
            pltpu.VMEM((2, 1, NE, GRP * CAP), f32),
            pltpu.VMEM((4, 128, 256), bf16),
            pltpu.VMEM((4, 128, 256), bf16),
            pltpu.VMEM((4, 128, 128), bf16),
            pltpu.VMEM((4, 128, 128), bf16),
            pltpu.VMEM((DOF, DOF), bf16),
            pltpu.VMEM((CHIPS * 128, DOF), bf16),
            pltpu.VMEM((2, CHIPS * 128, DOF // 2), bf16),
            pltpu.VMEM((CHIPS, CD, 128), f32),
            pltpu.VMEM((PARTS, CD, 128), f32),
            pltpu.VMEM((CHIPS, 8, 128), f32),
            pltpu.VMEM((PARTS, 8, 128), f32),
            pltpu.VMEM((4, 8, 128), f32),
            pltpu.VMEM((4, 8, 128), f32),
            pltpu.VMEM((NT, 128), f32),
            pltpu.VMEM((NT, 128), f32),
            pltpu.VMEM((2, PARTS, 8, 128), f32),
            pltpu.VMEM((2, CHIPS, 8, 128), f32),
            pltpu.VMEM((2, CHIPS, 8, 128), f32),
            pltpu.VMEM((8, DOF), f32),
            pltpu.VMEM((2, 8, DOF // 2), f32),
            pltpu.VMEM((CD, DOF), f32),
            pltpu.VMEM((2, CD, DOF // 2), f32),
            pltpu.VMEM((2, CD, DOF // 2), f32),
            pltpu.SemaphoreType.DMA((10,)),
            pltpu.SemaphoreType.DMA((6,)),
            pltpu.SemaphoreType.DMA((6,)),
            pltpu.SemaphoreType.DMA((3, 2)),
            pltpu.SemaphoreType.DMA((3, 2)),
        ],
        compiler_params=pltpu.CompilerParams(
            collective_id=0, has_side_effects=True, vmem_limit_bytes=60 * 2**20
        ),
    )(u, load, mass.reshape(1, DOF), offset.T, dofs, owner, basis, stiffness, k_table, s_table)
    return out[0], out[1]


def solution(mesh):
    in_specs = (
        P("harm", "grp"),
        P("harm", "grp"),
        P("grp"),
        P("grp", None, None, None),
        P("grp", None),
        P("grp", None),
        P("grp", None),
        P("grp", None, None),
        P("grp", None, None),
    )
    out_specs = (P("harm", "grp"), P("harm", "grp"))

    def run(*args):
        return tuple(local(*args))

    return jax.shard_map(run, mesh=mesh, in_specs=in_specs, out_specs=out_specs, check_vma=False)
```

```python
import math

import jax
import jax.numpy as jnp
import numpy as np
from jax import lax
from jax.experimental import pallas as pl
from jax.experimental.pallas import tpu as pltpu
from jax.sharding import PartitionSpec as P

HARM = 32
NT = 128
GRP = 32
PARTS = 16
CHIPS = 8
CD = 4
DOF = 512
JOINTS = 256
CAP = 24
NE = 16
f32, bf16, i32 = jnp.float32, jnp.bfloat16, jnp.int32
MESH = pl.DeviceIdType.MESH


def basis_tables():
    coef = np.arange(2 * HARM)
    harmonic = np.where(coef <= HARM, coef, coef - HARM)
    angle = 2.0 * math.pi * ((np.arange(NT)[:, None] * harmonic[None, :]) % NT) / NT
    synth = np.where(coef > HARM, np.sin(angle), np.cos(angle))
    travel = np.zeros((NT, NT), np.float32)
    travel[:, : 2 * HARM] = synth - synth[-1:]
    project = np.zeros((NT, NT), np.float32)
    project[: 2 * HARM] = (synth * np.where(coef == 0, 1.0, 2.0) / NT).T

    def split(x):
        high = x.astype(jnp.bfloat16)
        return [high, (x - high.astype(np.float32)).astype(jnp.bfloat16)]

    return np.stack(split(travel) + split(project))


def split2(x):
    high = x.astype(bf16).astype(f32)
    return high, x - high


def terms2(x):
    return jnp.concatenate(split2(x), axis=0).astype(bf16)


def terms3(x):
    high, rest = split2(x)
    mid, low = split2(rest)
    return jnp.concatenate([high, mid, low], axis=0).astype(bf16)


def mm(a, b):
    return lax.dot_general(a, b, (((1,), (0,)), ((), ())), preferred_element_type=f32)


def mm_t(a, b):
    return lax.dot_general(a, b, (((1,), (1,)), ((), ())), preferred_element_type=f32)


def select3(x, weights, product):
    n = x.shape[0]
    y = product(terms3(x), weights)
    return y[:n] + y[n : 2 * n] + y[2 * n :]


def kernel(
    u_hbm,
    load_hbm,
    mass_hbm,
    offset_hbm,
    dofs_hbm,
    owner_hbm,
    basis_hbm,
    stiff_hbm,
    k_hbm,
    s_hbm,
    out,
    u_v,
    load_v,
    mass_v,
    offset_v,
    dofs_v,
    owner_v,
    basis_v,
    stiff_v,
    table_v,
    near_hi,
    near_lo,
    far_hi,
    far_lo,
    perm,
    slots,
    slots_side,
    send1,
    recv1,
    send2,
    recv2,
    sendp,
    recvp,
    travel_v,
    total_v,
    sendg,
    recvg,
    recvg_side,
    fixed,
    fixed_side,
    base_v,
    base_side,
    u_side,
    local_sem,
    send_sem,
    recv_sem,
    side_send,
    side_recv,
):
    g = lax.axis_index("grp")
    h = lax.axis_index("harm")
    chip = lax.div(h, 2)
    core = lax.rem(h, 2)
    sides = (lax.rem(g + 1, GRP), lax.rem(g + GRP - 1, GRP))

    barrier = pltpu.get_barrier_semaphore()

    def greet(group, part):
        pl.semaphore_signal(barrier, inc=1, device_id=(group, part), device_id_type=MESH)

    source = 4 * (chip ^ (g >> 2) ^ 4)
    for k in range(4):
        greet(source + k, 2 * chip + 1 - core)
    for k in (4, 3, 5, 2, 6, 1, 7, 0):
        part = 2 * lax.rem(chip + k, CHIPS)
        for side in sides:
            greet(side, part + core)
        if k > 0:
            greet(g, part + core)
        greet(g, part + 1 - core)

    fetches = [
        pltpu.make_async_copy(src, dst, local_sem.at[i])
        for i, (src, dst) in enumerate(
            [
                (owner_hbm, owner_v),
                (dofs_hbm, dofs_v),
                (u_hbm, u_v),
                (load_hbm, load_v),
                (mass_hbm, mass_v),
                (offset_hbm, offset_v),
                (k_hbm, table_v.at[0]),
                (s_hbm, table_v.at[1]),
                (stiff_hbm, stiff_v),
                (basis_hbm, basis_v),
            ]
        )
    ]
    for fetch in fetches:
        fetch.start()

    fetches[0].wait()
    fetches[1].wait()
    owner = owner_v[...]
    own = jnp.where(lax.broadcasted_iota(i32, (GRP, JOINTS), 0) == owner, 1.0, 0.0)
    before = jnp.where(
        lax.broadcasted_iota(i32, (JOINTS, JOINTS), 0)
        < lax.broadcasted_iota(i32, (JOINTS, JOINTS), 1),
        1.0,
        0.0,
    )
    earlier = mm(own.astype(bf16), before.astype(bf16))
    rank = jnp.sum(earlier * own, axis=0, keepdims=True)
    tile = ((owner >> 2) ^ (g >> 2) ^ 4).astype(f32)
    lane = ((owner & 3) * CAP).astype(f32) + rank
    ones = jnp.ones((1, JOINTS), f32)
    dofs = dofs_v[...]
    row = lax.broadcasted_iota(i32, (128, DOF), 0)
    for m in range(DOF // 128):
        perm[m * 128 : (m + 1) * 128, :] = jnp.where(row == dofs - m * 128, 1.0, 0.0).astype(bf16)
    by_joint = jnp.concatenate(
        [
            jnp.concatenate([tile, lane, ones], axis=0),
            jnp.concatenate([tile, lane, -ones], axis=0),
        ],
        axis=1,
    )
    by_dof = mm_t(by_joint.astype(bf16), perm[...])
    slot_f = by_dof[0:1] * 128.0 + by_dof[1:2]
    slot = slot_f.astype(i32)
    sign = by_dof[2:3]
    for m in range(CHIPS):
        slots[m * 128 : (m + 1) * 128, :] = jnp.where(row == slot - m * 128, 1.0, 0.0).astype(bf16)

    fetches[2].wait()
    u0 = u_v[...]

    def to_slots(x, out):
        by_slot = select3(x, slots[...], mm_t)
        for m in range(CHIPS):
            for n in range(x.shape[0] // CD):
                out[m, n] = by_slot[n * CD : (n + 1) * CD, m * 128 : (m + 1) * 128]

    fetches[6].wait()
    fetches[7].wait()
    target = 4 * (chip ^ (g >> 2) ^ 4)
    at = lax.broadcasted_iota(i32, (8, 128), 1)
    quarters = [(at >= q * CAP) & (at < (q + 1) * CAP) for q in range(4)]
    for t in range(4):
        column = (target + t) * CAP
        begin = jnp.minimum(lax.div(column, 128), 4)
        packed = jnp.zeros((8, 128), f32)
        for q in range(4):
            rows = pl.ds(8 * (q % 2), 8)
            part = table_v[q // 2, 0, rows, pl.ds(pl.multiple_of(begin * 128, 128), 256)]
            shift = lax.rem(q * CAP - (column - begin * 128) + 512, 256)
            packed = jnp.where(quarters[q], pltpu.roll(part, shift, 1)[:, :128], packed)
        sendp[t] = packed

    fetches[8].wait()
    eye = lax.broadcasted_iota(i32, (128, 128), 0) == lax.broadcasted_iota(i32, (128, 128), 1)
    diagonals = []

    def store(hi, lo, i, at, block):
        high, low = split2(block)
        hi[i, :, at : at + 128] = high.astype(bf16)
        lo[i, :, at : at + 128] = low.astype(bf16)

    for i in range(4):
        own_block = stiff_v[i, 0]
        diagonals.append(jnp.sum(jnp.where(eye, own_block, 0.0), axis=0, keepdims=True))
        store(near_hi, near_lo, i, 0, jnp.where(eye, 0.0, own_block))
        store(near_hi, near_lo, i, 128, stiff_v[i, 2 if i < 2 else 1])
        store(far_hi, far_lo, i, 0, stiff_v[i, 1 if i < 2 else 2])
    kdiag = jnp.concatenate(diagonals, axis=1)
    coef = 4 * h + lax.broadcasted_iota(i32, (CD, DOF), 0)
    freq = jnp.where(coef <= HARM, coef, coef - HARM).astype(f32) * (1.0 / HARM)
    fetches[4].wait()
    net = kdiag - (freq * freq) * mass_v[...]
    precond = 1.0 / net
    signed = precond * sign
    to_slots(jnp.concatenate([u0 * sign, precond], axis=0), send1)
    fixed[...] = jnp.concatenate([signed, jnp.broadcast_to(slot_f, (CD, DOF))], axis=0)
    fetches[5].wait()
    offset = offset_v[...]

    def block(u, i):
        return u[:, i * 128 : (i + 1) * 128]

    def nearer(i, k):
        return jnp.abs(offset[k : k + 1, i : i + 1]) == 1

    def apply(lhs, hi, lo):
        terms = terms2(lhs)
        a = mm_t(terms, hi)
        b = mm_t(terms, lo)
        return a[:CD] + (a[CD:] + b[:CD])

    def near_product(u):
        parts = []
        for i in range(4):
            if i < 2:
                other = jnp.where(nearer(i, 1), block(u, i + 1), block(u, i + 2))
            else:
                other = jnp.where(nearer(i, 0), block(u, i - 1), block(u, i - 2))
            lhs = jnp.concatenate([block(u, i), other], axis=1)
            parts.append(apply(lhs, near_hi[i], near_lo[i]))
        return jnp.concatenate(parts, axis=1)

    def far_product(u, low, high):
        low = jnp.where(g > 0, low, 0.0)
        high = jnp.where(g < GRP - 1, high, 0.0)
        others = [
            jnp.where(nearer(0, 0), block(low, 1), block(low, 0)),
            jnp.where(nearer(1, 0), block(u, 0), block(low, 1)),
            jnp.where(nearer(2, 1), block(u, 3), block(high, 0)),
            jnp.where(nearer(3, 1), block(high, 0), block(high, 1)),
        ]
        return jnp.concatenate(
            [apply(others[i], far_hi[i], far_lo[i]) for i in range(4)], axis=1
        )

    fetches[3].wait()
    load = load_v[...]
    part = load - near_product(u0)
    pl.semaphore_wait(barrier, PARTS - 1 + 2 * CHIPS + 4)

    def send_sides(n, src, dst):
        copies = [
            pltpu.make_async_remote_copy(
                src_ref=src.at[:, 256:512] if k == 0 else src.at[:, 0:256],
                dst_ref=dst.at[k],
                send_sem=side_send.at[n, k],
                recv_sem=side_recv.at[n, k],
                device_id=(side, h),
                device_id_type=MESH,
            )
            for k, side in enumerate(sides)
        ]
        for copy in copies:
            copy.start()
        return copies

    def send_parts(n, src, dst):
        for k in (8, 7, 9, 6, 10, 5, 11, 4, 12, 3, 13, 2, 14, 1, 15):
            to = lax.rem(h + k, PARTS)
            pltpu.make_async_remote_copy(
                src_ref=src.at[lax.div(to, 2)],
                dst_ref=dst.at[h],
                send_sem=send_sem.at[n],
                recv_sem=recv_sem.at[n],
                device_id=(g, to),
                device_id_type=MESH,
            ).start()
        dst[h] = src[chip]

    def settle(ref, sem):
        pltpu.make_async_copy(ref, ref, sem).wait()

    halo0 = send_sides(0, u_v, u_side)
    for t in range(4):
        pltpu.make_async_remote_copy(
            src_ref=sendp.at[t],
            dst_ref=recvp.at[lax.rem(g, 4)],
            send_sem=send_sem.at[2],
            recv_sem=recv_sem.at[2],
            device_id=(target + t, 2 * chip + 1 - core),
            device_id_type=MESH,
        ).start()
    send_parts(0, send1, recv1)
    halof = send_sides(1, fixed, fixed_side)


    for copy in halo0:
        copy.wait_recv()
    base = precond * (part - far_product(u0, u_side[0], u_side[1]))
    to_slots(base * sign, send2)
    send_parts(1, send2, recv2)
    base_v[...] = base
    halob = send_sides(2, base_v, base_side)

    for copy in halof:
        copy.wait_recv()
    row = lax.broadcasted_iota(i32, (128, DOF // 2), 0)
    for k in range(2):
        slot_side = fixed_side[k, CD : CD + 1, :].astype(i32)
        for m in range(CHIPS):
            slots_side[k, m * 128 : (m + 1) * 128, :] = jnp.where(
                row == slot_side - m * 128, 1.0, 0.0
            ).astype(bf16)

    fetches[9].wait()
    settle(recv1.at[pl.ds(0, PARTS - 1)], recv_sem.at[0])
    settle(recvp, recv_sem.at[2])
    table = []
    for r in range(4):
        rows = jnp.zeros((8, 128), f32)
        for q in range(4):
            part = recvp[q]
            if q != r:
                part = pltpu.roll(part, ((q - r) * CAP) % 128, 1)
            rows = jnp.where(quarters[q], part, rows)
        table.append(rows)
    k_slot = jnp.concatenate(table[:2], axis=0)
    s_slot = jnp.concatenate(table[2:], axis=0)
    minus_s = -s_slot

    def forces(x, n):
        high, low = split2(x.reshape(2 * HARM, 128))
        high, low = high.astype(bf16), low.astype(bf16)
        high_t, low_t = basis_v[0, :, : 2 * HARM], basis_v[1, :, : 2 * HARM]
        travel_v[...] = mm(high_t, high) + (mm(low_t, high) + mm(high_t, low))

        def samples(i, p):
            at = pl.multiple_of(8 * i, 8)
            travel = travel_v[pl.ds(at, 8), :]
            sums = []
            for j in range(8):
                m = k_slot * travel[j : j + 1, :]
                p = jnp.minimum(jnp.maximum(p, minus_s - m), s_slot - m)
                sums.append(jnp.sum(p + m, axis=0, keepdims=True))
            total_v[pl.ds(at, 8), :] = jnp.concatenate(sums, axis=0)
            return p

        lax.fori_loop(0, NT // 8, samples, jnp.zeros((NE, 128), f32), unroll=4)
        high, low = split2(total_v[...])
        high, low = high.astype(bf16), low.astype(bf16)
        high_t, low_t = basis_v[2, : 2 * HARM], basis_v[3, : 2 * HARM]
        coefs = mm(high_t, high) + (mm(low_t, high) + mm(high_t, low))
        sendg[n] = coefs.reshape(PARTS, CD, 128)
        for k in (4, 3, 5, 2, 6, 1, 7, 0):
            to = 2 * lax.rem(chip + k, CHIPS) + core
            if n == 0:
                for d, side in enumerate(sides):
                    pltpu.make_async_remote_copy(
                        src_ref=sendg.at[0, to],
                        dst_ref=recvg_side.at[d, chip],
                        send_sem=send_sem.at[5],
                        recv_sem=recv_sem.at[5],
                        device_id=(side, to),
                        device_id_type=MESH,
                    ).start()
            if k > 0:
                pltpu.make_async_remote_copy(
                    src_ref=sendg.at[n, to],
                    dst_ref=recvg.at[n, chip],
                    send_sem=send_sem.at[3 + n],
                    recv_sem=recv_sem.at[3 + n],
                    device_id=(g, to),
                    device_id_type=MESH,
                ).start()
        recvg[n, chip] = sendg[n, h]

    def to_dofs(x, weights):
        lanes = jnp.concatenate([x[m] for m in range(CHIPS)], axis=1)
        return select3(lanes, weights, mm)

    forces(recv1[:, 0], 0)
    settle(recv2.at[pl.ds(0, PARTS - 1)], recv_sem.at[1])
    forces(recv2[:, 0] - recv1[:, 1] * sendg[0], 1)

    settle(recvg.at[0, pl.ds(0, CHIPS - 1)], recv_sem.at[3])
    u1 = base - signed * to_dofs(recvg[0], slots[...])
    part = near_product(u1) + net * u1 - load
    for copy in halob:
        copy.wait_recv()
    settle(recvg_side, recv_sem.at[5])
    low, high = [
        base_side[k] - fixed_side[k, :CD, :] * to_dofs(recvg_side[k], slots_side[k])
        for k in range(2)
    ]
    part = part + far_product(u1, low, high)
    settle(recvg.at[1, pl.ds(0, CHIPS - 1)], recv_sem.at[4])
    residual = part + sign * to_dofs(recvg[1], slots[...])
    out[1] = residual
    out[0] = u1 - precond * residual

    for copy in halo0 + halof + halob:
        copy.wait_send()
    settle(recv1.at[pl.ds(0, PARTS - 1)], send_sem.at[0])
    settle(recv2.at[pl.ds(0, PARTS - 1)], send_sem.at[1])
    settle(recvp, send_sem.at[2])
    for n in range(2):
        settle(recvg.at[n, pl.ds(0, CHIPS - 1)], send_sem.at[3 + n])
    settle(recvg_side, send_sem.at[5])


def local(u, load, mass, stiffness, offset, dofs, owner, k_table, s_table):
    basis = jnp.asarray(basis_tables())
    hbm = pl.BlockSpec(memory_space=pltpu.HBM)
    vmem = pl.BlockSpec(memory_space=pltpu.VMEM)
    out = pl.pallas_call(
        kernel,
        out_shape=pltpu.VMEM((2, CD, DOF), f32),
        in_specs=[hbm] * 10,
        out_specs=vmem,
        scratch_shapes=[
            pltpu.VMEM((CD, DOF), f32),
            pltpu.VMEM((CD, DOF), f32),
            pltpu.VMEM((1, DOF), f32),
            pltpu.VMEM((2, 4), i32),
            pltpu.VMEM((1, DOF), i32),
            pltpu.VMEM((1, JOINTS), i32),
            pltpu.VMEM((4, 128, 128), bf16),
            pltpu.VMEM((4, 3, 128, 128), f32),
            pltpu.VMEM((2, 1, NE, GRP * CAP), f32),
            pltpu.VMEM((4, 128, 256), bf16),
            pltpu.VMEM((4, 128, 256), bf16),
            pltpu.VMEM((4, 128, 128), bf16),
            pltpu.VMEM((4, 128, 128), bf16),
            pltpu.VMEM((DOF, DOF), bf16),
            pltpu.VMEM((CHIPS * 128, DOF), bf16),
            pltpu.VMEM((2, CHIPS * 128, DOF // 2), bf16),
            pltpu.VMEM((CHIPS, 2, CD, 128), f32),
            pltpu.VMEM((PARTS, 2, CD, 128), f32),
            pltpu.VMEM((CHIPS, 1, CD, 128), f32),
            pltpu.VMEM((PARTS, 1, CD, 128), f32),
            pltpu.VMEM((4, 8, 128), f32),
            pltpu.VMEM((4, 8, 128), f32),
            pltpu.VMEM((NT, 128), f32),
            pltpu.VMEM((NT, 128), f32),
            pltpu.VMEM((2, PARTS, CD, 128), f32),
            pltpu.VMEM((2, CHIPS, CD, 128), f32),
            pltpu.VMEM((2, CHIPS, CD, 128), f32),
            pltpu.VMEM((8, DOF), f32),
            pltpu.VMEM((2, 8, DOF // 2), f32),
            pltpu.VMEM((CD, DOF), f32),
            pltpu.VMEM((2, CD, DOF // 2), f32),
            pltpu.VMEM((2, CD, DOF // 2), f32),
            pltpu.SemaphoreType.DMA((10,)),
            pltpu.SemaphoreType.DMA((6,)),
            pltpu.SemaphoreType.DMA((6,)),
            pltpu.SemaphoreType.DMA((3, 2)),
            pltpu.SemaphoreType.DMA((3, 2)),
        ],
        compiler_params=pltpu.CompilerParams(
            collective_id=0, has_side_effects=True, vmem_limit_bytes=60 * 2**20
        ),
    )(u, load, mass.reshape(1, DOF), offset.T, dofs, owner, basis, stiffness, k_table, s_table)
    return out[0], out[1]


def solution(mesh):
    in_specs = (
        P("harm", "grp"),
        P("harm", "grp"),
        P("grp"),
        P("grp", None, None, None),
        P("grp", None),
        P("grp", None),
        P("grp", None),
        P("grp", None, None),
        P("grp", None, None),
    )
    out_specs = (P("harm", "grp"), P("harm", "grp"))

    def run(*args):
        return tuple(local(*args))

    return jax.shard_map(run, mesh=mesh, in_specs=in_specs, out_specs=out_specs, check_vma=False)
```

```python
import math

import jax
import jax.numpy as jnp
import numpy as np
from jax import lax
from jax.experimental import pallas as pl
from jax.experimental.pallas import tpu as pltpu
from jax.sharding import PartitionSpec as P

HARM = 32
NT = 128
GRP = 32
PARTS = 16
CHIPS = 8
CD = 4
DOF = 512
JOINTS = 256
CAP = 24
NE = 16
f32, bf16, i32 = jnp.float32, jnp.bfloat16, jnp.int32
MESH = pl.DeviceIdType.MESH


def basis_tables():
    coef = np.arange(2 * HARM)
    harmonic = np.where(coef <= HARM, coef, coef - HARM)
    angle = 2.0 * math.pi * ((np.arange(NT)[:, None] * harmonic[None, :]) % NT) / NT
    synth = np.where(coef > HARM, np.sin(angle), np.cos(angle))
    travel = np.zeros((NT, NT), np.float32)
    travel[:, : 2 * HARM] = synth - synth[-1:]
    project = np.zeros((NT, NT), np.float32)
    project[: 2 * HARM] = (synth * np.where(coef == 0, 1.0, 2.0) / NT).T

    def split(x):
        high = x.astype(jnp.bfloat16)
        return [high, (x - high.astype(np.float32)).astype(jnp.bfloat16)]

    return np.stack(split(travel) + split(project))


def split2(x):
    high = x.astype(bf16).astype(f32)
    return high, x - high


def terms2(x):
    return jnp.concatenate(split2(x), axis=0).astype(bf16)


def terms3(x):
    high, rest = split2(x)
    mid, low = split2(rest)
    return jnp.concatenate([high, mid, low], axis=0).astype(bf16)


def mm(a, b):
    return lax.dot_general(a, b, (((1,), (0,)), ((), ())), preferred_element_type=f32)


def mm_t(a, b):
    return lax.dot_general(a, b, (((1,), (1,)), ((), ())), preferred_element_type=f32)


def select3(x, weights, product):
    n = x.shape[0]
    y = product(terms3(x), weights)
    return y[:n] + y[n : 2 * n] + y[2 * n :]


def kernel(
    u_hbm,
    load_hbm,
    mass_hbm,
    offset_hbm,
    dofs_hbm,
    owner_hbm,
    basis_hbm,
    stiff_hbm,
    k_hbm,
    s_hbm,
    out,
    u_v,
    load_v,
    mass_v,
    offset_v,
    dofs_v,
    owner_v,
    basis_v,
    stiff_v,
    table_v,
    near_hi,
    near_lo,
    far_hi,
    far_lo,
    perm,
    slots,
    slots_side,
    send1,
    recv1,
    send2,
    recv2,
    sendp,
    recvp,
    travel_v,
    total_v,
    sendg,
    recvg,
    recvg_side,
    fixed,
    fixed_side,
    base_v,
    base_side,
    u_side,
    local_sem,
    send_sem,
    recv_sem,
    side_send,
    side_recv,
    ready,
):
    g = lax.axis_index("grp")
    h = lax.axis_index("harm")
    chip = lax.div(h, 2)
    core = lax.rem(h, 2)
    sides = (lax.rem(g + 1, GRP), lax.rem(g + GRP - 1, GRP))

    far = [(4 * (chip ^ (g >> 2) ^ 4) + t, 2 * chip + 1 - core) for t in range(4)]

    def place(part):
        y = part >> 1
        return 2 * jnp.where(y < 4, y, 11 - y) + (part & 1)

    def far_place(group, part):
        return 8 * (group & 7) + 2 * (group >> 3) + (part & 1)

    mates = [lax.rem(h + k, PARTS) for k in (8, 7, 9, 6, 10, 5, 11, 4, 12, 3, 13, 2, 14, 1, 15)]
    later_mate = [place(part) > place(h) for part in mates]
    exists = (g < GRP - 1, g > 0)
    later_side = [there & ((side & 7) > (g & 7)) for there, side in zip(exists, sides)]
    earlier_side = [there & ((side & 7) < (g & 7)) for there, side in zip(exists, sides)]
    later_far = [far_place(*peer) > far_place(g, h) for peer in far]
    n_mates = PARTS - 1 - place(h)
    n_sides = sum(later.astype(i32) for later in later_side)
    n_before = sum(earlier.astype(i32) for earlier in earlier_side)
    n_far = sum(later.astype(i32) for later in later_far)
    barrier = pltpu.get_barrier_semaphore()

    def signal(sem, group, part):
        pl.semaphore_signal(sem, inc=1, device_id=(group, part), device_id_type=MESH)

    def tell(later, sems):
        def when(flag, peers, sem):
            @pl.when(flag)
            def _():
                for group, part in peers:
                    signal(sem, group, part)

        side_flags = later_side if later else earlier_side
        for d, side in enumerate(sides):
            when(side_flags[d], [(side, h)], sems[1])
        for flag, peer in zip(later_far, far):
            when(flag if later else jnp.logical_not(flag), [peer], sems[2])
        for flag, part in zip(later_mate, mates):
            when(flag if later else jnp.logical_not(flag), [(g, part)], sems[0])
        for d, side in enumerate(sides):
            others = [(side, 2 * lax.rem(chip + k, CHIPS) + core) for k in (4, 3, 5, 2, 6, 1, 7)]
            when(side_flags[d], others, sems[3])

    tell(True, [barrier] * 4)

    fetches = [
        pltpu.make_async_copy(src, dst, local_sem.at[i])
        for i, (src, dst) in enumerate(
            [
                (owner_hbm, owner_v),
                (dofs_hbm, dofs_v),
                (u_hbm, u_v),
                (load_hbm, load_v),
                (mass_hbm, mass_v),
                (offset_hbm, offset_v),
                (k_hbm, table_v.at[0]),
                (s_hbm, table_v.at[1]),
                (stiff_hbm, stiff_v),
                (basis_hbm, basis_v),
            ]
        )
    ]
    for fetch in fetches:
        fetch.start()

    def await_some(sem, n):
        @pl.when(n > 0)
        def _():
            pl.semaphore_wait(sem, n)

    await_some(barrier, (PARTS - 1 - n_mates) + CHIPS * n_before + (4 - n_far))
    tell(False, [ready.at[i] for i in range(4)])

    def start_if(copies, flags):
        for copy, flag in zip(copies, flags):
            pl.when(flag)(copy.start)

    def wait_sides(copies):
        for copy, there in zip(copies, (g > 0, g < GRP - 1)):
            pl.when(there)(copy.wait_recv)

    for k, there in enumerate((g > 0, g < GRP - 1)):

        @pl.when(jnp.logical_not(there))
        def _():
            for ref in (u_side, fixed_side, base_side, recvg_side):
                ref[k] = jnp.zeros(ref.shape[1:], f32)

    def side_copies(n, src, dst):
        return [
            pltpu.make_async_remote_copy(
                src_ref=src.at[:, 256:512] if k == 0 else src.at[:, 0:256],
                dst_ref=dst.at[k],
                send_sem=side_send.at[n, k],
                recv_sem=side_recv.at[n, k],
                device_id=(side, h),
                device_id_type=MESH,
            )
            for k, side in enumerate(sides)
        ]

    def send_sides(n, src, dst):
        copies = side_copies(n, src, dst)
        start_if(copies, exists)
        return copies

    def send_parts(n, src, dst):
        for to in mates:
            pltpu.make_async_remote_copy(
                src_ref=src.at[lax.div(to, 2)],
                dst_ref=dst.at[h],
                send_sem=send_sem.at[n],
                recv_sem=recv_sem.at[n],
                device_id=(g, to),
                device_id_type=MESH,
            ).start()
        dst[h] = src[chip]

    def settle(ref, sem):
        pltpu.make_async_copy(ref, ref, sem).wait()

    def settle_sides(sems, flags):
        for d, there in enumerate(flags):

            @pl.when(there)
            def _():
                settle(recvg_side.at[d], sems.at[5 + d])

    halo0 = side_copies(0, u_hbm, u_side)
    start_if(halo0, earlier_side)

    fetches[0].wait()
    fetches[1].wait()
    owner = owner_v[...]
    own = jnp.where(lax.broadcasted_iota(i32, (GRP, JOINTS), 0) == owner, 1.0, 0.0)
    before = jnp.where(
        lax.broadcasted_iota(i32, (JOINTS, JOINTS), 0)
        < lax.broadcasted_iota(i32, (JOINTS, JOINTS), 1),
        1.0,
        0.0,
    )
    earlier = mm(own.astype(bf16), before.astype(bf16))
    rank = jnp.sum(earlier * own, axis=0, keepdims=True)
    tile = ((owner >> 2) ^ (g >> 2) ^ 4).astype(f32)
    lane = ((owner & 3) * CAP).astype(f32) + rank
    ones = jnp.ones((1, JOINTS), f32)
    dofs = dofs_v[...]
    row = lax.broadcasted_iota(i32, (128, DOF), 0)
    for m in range(DOF // 128):
        perm[m * 128 : (m + 1) * 128, :] = jnp.where(row == dofs - m * 128, 1.0, 0.0).astype(bf16)
    by_joint = jnp.concatenate(
        [
            jnp.concatenate([tile, lane, ones], axis=0),
            jnp.concatenate([tile, lane, -ones], axis=0),
        ],
        axis=1,
    )
    by_dof = mm_t(by_joint.astype(bf16), perm[...])
    slot_f = by_dof[0:1] * 128.0 + by_dof[1:2]
    slot = slot_f.astype(i32)
    sign = by_dof[2:3]
    for m in range(CHIPS):
        slots[m * 128 : (m + 1) * 128, :] = jnp.where(row == slot - m * 128, 1.0, 0.0).astype(bf16)

    fetches[2].wait()
    u0 = u_v[...]

    def to_slots(x, out):
        by_slot = select3(x, slots[...], mm_t)
        for m in range(CHIPS):
            for n in range(x.shape[0] // CD):
                out[m, n] = by_slot[n * CD : (n + 1) * CD, m * 128 : (m + 1) * 128]

    fetches[6].wait()
    fetches[7].wait()
    at = lax.broadcasted_iota(i32, (8, 128), 1)
    quarters = [(at >= q * CAP) & (at < (q + 1) * CAP) for q in range(4)]
    for t in range(4):
        column = far[t][0] * CAP
        begin = jnp.minimum(lax.div(column, 128), 4)
        packed = jnp.zeros((8, 128), f32)
        for q in range(4):
            rows = pl.ds(8 * (q % 2), 8)
            part = table_v[q // 2, 0, rows, pl.ds(pl.multiple_of(begin * 128, 128), 256)]
            shift = lax.rem(q * CAP - (column - begin * 128) + 512, 256)
            packed = jnp.where(quarters[q], pltpu.roll(part, shift, 1)[:, :128], packed)
        sendp[t] = packed
    tables = [
        pltpu.make_async_remote_copy(
            src_ref=sendp.at[t],
            dst_ref=recvp.at[lax.rem(g, 4)],
            send_sem=send_sem.at[2],
            recv_sem=recv_sem.at[2],
            device_id=peer,
            device_id_type=MESH,
        )
        for t, peer in enumerate(far)
    ]
    start_if(tables, [jnp.logical_not(later) for later in later_far])

    fetches[8].wait()
    eye = lax.broadcasted_iota(i32, (128, 128), 0) == lax.broadcasted_iota(i32, (128, 128), 1)
    diagonals = []

    def store(hi, lo, i, at, block):
        high, low = split2(block)
        hi[i, :, at : at + 128] = high.astype(bf16)
        lo[i, :, at : at + 128] = low.astype(bf16)

    for i in range(4):
        own_block = stiff_v[i, 0]
        diagonals.append(jnp.sum(jnp.where(eye, own_block, 0.0), axis=0, keepdims=True))
        store(near_hi, near_lo, i, 0, jnp.where(eye, 0.0, own_block))
        store(near_hi, near_lo, i, 128, stiff_v[i, 2 if i < 2 else 1])
        store(far_hi, far_lo, i, 0, stiff_v[i, 1 if i < 2 else 2])
    kdiag = jnp.concatenate(diagonals, axis=1)
    coef = 4 * h + lax.broadcasted_iota(i32, (CD, DOF), 0)
    freq = jnp.where(coef <= HARM, coef, coef - HARM).astype(f32) * (1.0 / HARM)
    fetches[4].wait()
    net = kdiag - (freq * freq) * mass_v[...]
    precond = 1.0 / net
    signed = precond * sign
    to_slots(jnp.concatenate([u0 * sign, precond], axis=0), send1)
    fixed[...] = jnp.concatenate([signed, jnp.broadcast_to(slot_f, (CD, DOF))], axis=0)
    fetches[5].wait()
    offset = offset_v[...]

    def block(u, i):
        return u[:, i * 128 : (i + 1) * 128]

    def nearer(i, k):
        return jnp.abs(offset[k : k + 1, i : i + 1]) == 1

    def apply(lhs, hi, lo):
        terms = terms2(lhs)
        a = mm_t(terms, hi)
        b = mm_t(terms, lo)
        return a[:CD] + (a[CD:] + b[:CD])

    def near_product(u):
        parts = []
        for i in range(4):
            if i < 2:
                other = jnp.where(nearer(i, 1), block(u, i + 1), block(u, i + 2))
            else:
                other = jnp.where(nearer(i, 0), block(u, i - 1), block(u, i - 2))
            lhs = jnp.concatenate([block(u, i), other], axis=1)
            parts.append(apply(lhs, near_hi[i], near_lo[i]))
        return jnp.concatenate(parts, axis=1)

    def far_product(u, low, high):
        others = [
            jnp.where(nearer(0, 0), block(low, 1), block(low, 0)),
            jnp.where(nearer(1, 0), block(u, 0), block(low, 1)),
            jnp.where(nearer(2, 1), block(u, 3), block(high, 0)),
            jnp.where(nearer(3, 1), block(high, 0), block(high, 1)),
        ]
        return jnp.concatenate(
            [apply(others[i], far_hi[i], far_lo[i]) for i in range(4)], axis=1
        )

    fetches[3].wait()
    load = load_v[...]
    part = load - near_product(u0)
    await_some(ready.at[0], n_mates)
    send_parts(0, send1, recv1)
    await_some(ready.at[1], n_sides)
    start_if(halo0, later_side)
    halof = send_sides(1, fixed, fixed_side)
    await_some(ready.at[2], n_far)
    start_if(tables, later_far)


    wait_sides(halo0)
    base = precond * (part - far_product(u0, u_side[0], u_side[1]))
    to_slots(base * sign, send2)
    send_parts(1, send2, recv2)
    base_v[...] = base
    halob = send_sides(2, base_v, base_side)

    fetches[9].wait()
    settle(recv1.at[pl.ds(0, PARTS - 1)], recv_sem.at[0])
    settle(recvp, recv_sem.at[2])
    table = []
    for r in range(4):
        rows = jnp.zeros((8, 128), f32)
        for q in range(4):
            part = recvp[q]
            if q != r:
                part = pltpu.roll(part, ((q - r) * CAP) % 128, 1)
            rows = jnp.where(quarters[q], part, rows)
        table.append(rows)
    k_slot = jnp.concatenate(table[:2], axis=0)
    s_slot = jnp.concatenate(table[2:], axis=0)
    minus_s = -s_slot

    def forces(x, n):
        high, low = split2(x.reshape(2 * HARM, 128))
        high, low = high.astype(bf16), low.astype(bf16)
        high_t, low_t = basis_v[0, :, : 2 * HARM], basis_v[1, :, : 2 * HARM]
        travel_v[...] = mm(high_t, high) + (mm(low_t, high) + mm(high_t, low))

        def samples(i, p):
            at = pl.multiple_of(8 * i, 8)
            travel = travel_v[pl.ds(at, 8), :]
            sums = []
            for j in range(8):
                m = k_slot * travel[j : j + 1, :]
                p = jnp.minimum(jnp.maximum(p, minus_s - m), s_slot - m)
                sums.append(jnp.sum(p + m, axis=0, keepdims=True))
            total_v[pl.ds(at, 8), :] = jnp.concatenate(sums, axis=0)
            return p

        lax.fori_loop(0, NT // 8, samples, jnp.zeros((NE, 128), f32), unroll=4)
        high, low = split2(total_v[...])
        high, low = high.astype(bf16), low.astype(bf16)
        high_t, low_t = basis_v[2, : 2 * HARM], basis_v[3, : 2 * HARM]
        coefs = mm(high_t, high) + (mm(low_t, high) + mm(high_t, low))
        sendg[n] = coefs.reshape(PARTS, CD, 128)
        if n == 0:
            await_some(ready.at[3], (CHIPS - 1) * n_sides)
        for k in (4, 3, 5, 2, 6, 1, 7, 0):
            to = 2 * lax.rem(chip + k, CHIPS) + core
            if n == 0:
                copies = [
                    pltpu.make_async_remote_copy(
                        src_ref=sendg.at[0, to],
                        dst_ref=recvg_side.at[d, chip],
                        send_sem=send_sem.at[5 + d],
                        recv_sem=recv_sem.at[5 + d],
                        device_id=(side, to),
                        device_id_type=MESH,
                    )
                    for d, side in enumerate(sides)
                ]
                start_if(copies, exists)
            if k > 0:
                pltpu.make_async_remote_copy(
                    src_ref=sendg.at[n, to],
                    dst_ref=recvg.at[n, chip],
                    send_sem=send_sem.at[3 + n],
                    recv_sem=recv_sem.at[3 + n],
                    device_id=(g, to),
                    device_id_type=MESH,
                ).start()
        recvg[n, chip] = sendg[n, h]

    def to_dofs(x, weights):
        lanes = jnp.concatenate([x[m] for m in range(CHIPS)], axis=1)
        return select3(lanes, weights, mm)

    forces(recv1[:, 0], 0)
    settle(recv2.at[pl.ds(0, PARTS - 1)], recv_sem.at[1])
    forces(recv2[:, 0] - recv1[:, 1] * sendg[0], 1)

    wait_sides(halof)
    row = lax.broadcasted_iota(i32, (128, DOF // 2), 0)
    for k in range(2):
        slot_side = fixed_side[k, CD : CD + 1, :].astype(i32)
        for m in range(CHIPS):
            slots_side[k, m * 128 : (m + 1) * 128, :] = jnp.where(
                row == slot_side - m * 128, 1.0, 0.0
            ).astype(bf16)

    settle(recvg.at[0, pl.ds(0, CHIPS - 1)], recv_sem.at[3])
    u1 = base - signed * to_dofs(recvg[0], slots[...])
    part = near_product(u1) + net * u1 - load
    wait_sides(halob)
    settle_sides(recv_sem, (g > 0, g < GRP - 1))
    low, high = [
        base_side[k] - fixed_side[k, :CD, :] * to_dofs(recvg_side[k], slots_side[k])
        for k in range(2)
    ]
    part = part + far_product(u1, low, high)
    settle(recvg.at[1, pl.ds(0, CHIPS - 1)], recv_sem.at[4])
    residual = part + sign * to_dofs(recvg[1], slots[...])
    out[1] = residual
    out[0] = u1 - precond * residual

    for copies in (halo0, halof, halob):
        for copy, there in zip(copies, exists):
            pl.when(there)(copy.wait_send)
    settle(recv1.at[pl.ds(0, PARTS - 1)], send_sem.at[0])
    settle(recv2.at[pl.ds(0, PARTS - 1)], send_sem.at[1])
    settle(recvp, send_sem.at[2])
    for n in range(2):
        settle(recvg.at[n, pl.ds(0, CHIPS - 1)], send_sem.at[3 + n])
    settle_sides(send_sem, exists)


def local(u, load, mass, stiffness, offset, dofs, owner, k_table, s_table):
    basis = jnp.asarray(basis_tables())
    hbm = pl.BlockSpec(memory_space=pltpu.HBM)
    vmem = pl.BlockSpec(memory_space=pltpu.VMEM)
    out = pl.pallas_call(
        kernel,
        out_shape=pltpu.VMEM((2, CD, DOF), f32),
        in_specs=[hbm] * 10,
        out_specs=vmem,
        scratch_shapes=[
            pltpu.VMEM((CD, DOF), f32),
            pltpu.VMEM((CD, DOF), f32),
            pltpu.VMEM((1, DOF), f32),
            pltpu.VMEM((2, 4), i32),
            pltpu.VMEM((1, DOF), i32),
            pltpu.VMEM((1, JOINTS), i32),
            pltpu.VMEM((4, 128, 128), bf16),
            pltpu.VMEM((4, 3, 128, 128), f32),
            pltpu.VMEM((2, 1, NE, GRP * CAP), f32),
            pltpu.VMEM((4, 128, 256), bf16),
            pltpu.VMEM((4, 128, 256), bf16),
            pltpu.VMEM((4, 128, 128), bf16),
            pltpu.VMEM((4, 128, 128), bf16),
            pltpu.VMEM((DOF, DOF), bf16),
            pltpu.VMEM((CHIPS * 128, DOF), bf16),
            pltpu.VMEM((2, CHIPS * 128, DOF // 2), bf16),
            pltpu.VMEM((CHIPS, 2, CD, 128), f32),
            pltpu.VMEM((PARTS, 2, CD, 128), f32),
            pltpu.VMEM((CHIPS, 1, CD, 128), f32),
            pltpu.VMEM((PARTS, 1, CD, 128), f32),
            pltpu.VMEM((4, 8, 128), f32),
            pltpu.VMEM((4, 8, 128), f32),
            pltpu.VMEM((NT, 128), f32),
            pltpu.VMEM((NT, 128), f32),
            pltpu.VMEM((2, PARTS, CD, 128), f32),
            pltpu.VMEM((2, CHIPS, CD, 128), f32),
            pltpu.VMEM((2, CHIPS, CD, 128), f32),
            pltpu.VMEM((8, DOF), f32),
            pltpu.VMEM((2, 8, DOF // 2), f32),
            pltpu.VMEM((CD, DOF), f32),
            pltpu.VMEM((2, CD, DOF // 2), f32),
            pltpu.VMEM((2, CD, DOF // 2), f32),
            pltpu.SemaphoreType.DMA((10,)),
            pltpu.SemaphoreType.DMA((7,)),
            pltpu.SemaphoreType.DMA((7,)),
            pltpu.SemaphoreType.DMA((3, 2)),
            pltpu.SemaphoreType.DMA((3, 2)),
            pltpu.SemaphoreType.REGULAR((4,)),
        ],
        compiler_params=pltpu.CompilerParams(
            collective_id=0, has_side_effects=True, vmem_limit_bytes=60 * 2**20
        ),
    )(u, load, mass.reshape(1, DOF), offset.T, dofs, owner, basis, stiffness, k_table, s_table)
    return out[0], out[1]


def solution(mesh):
    in_specs = (
        P("harm", "grp"),
        P("harm", "grp"),
        P("grp"),
        P("grp", None, None, None),
        P("grp", None),
        P("grp", None),
        P("grp", None),
        P("grp", None, None),
        P("grp", None, None),
    )
    out_specs = (P("harm", "grp"), P("harm", "grp"))

    def run(*args):
        return tuple(local(*args))

    return jax.shard_map(run, mesh=mesh, in_specs=in_specs, out_specs=out_specs, check_vma=False)
```

```python
import math

import jax
import jax.numpy as jnp
import numpy as np
from jax import lax
from jax.experimental import pallas as pl
from jax.experimental.pallas import tpu as pltpu
from jax.sharding import PartitionSpec as P

HARM = 32
NT = 128
GRP = 32
PARTS = 16
CHIPS = 8
CD = 4
DOF = 512
JOINTS = 256
CAP = 24
NE = 16
f32, bf16, i32 = jnp.float32, jnp.bfloat16, jnp.int32
MESH = pl.DeviceIdType.MESH


def basis_tables():
    coef = np.arange(2 * HARM)
    harmonic = np.where(coef <= HARM, coef, coef - HARM)
    angle = 2.0 * math.pi * ((np.arange(NT)[:, None] * harmonic[None, :]) % NT) / NT
    synth = np.where(coef > HARM, np.sin(angle), np.cos(angle))
    travel = np.zeros((NT, NT), np.float32)
    travel[:, : 2 * HARM] = synth - synth[-1:]
    project = np.zeros((NT, NT), np.float32)
    project[: 2 * HARM] = (synth * np.where(coef == 0, 1.0, 2.0) / NT).T

    def split(x):
        high = x.astype(jnp.bfloat16)
        return [high, (x - high.astype(np.float32)).astype(jnp.bfloat16)]

    return np.stack(split(travel) + split(project))


def split2(x):
    high = x.astype(bf16).astype(f32)
    return high, x - high


def terms2(x):
    return jnp.concatenate(split2(x), axis=0).astype(bf16)


def terms3(x):
    high, rest = split2(x)
    mid, low = split2(rest)
    return jnp.concatenate([high, mid, low], axis=0).astype(bf16)


def mm(a, b):
    return lax.dot_general(a, b, (((1,), (0,)), ((), ())), preferred_element_type=f32)


def mm_t(a, b):
    return lax.dot_general(a, b, (((1,), (1,)), ((), ())), preferred_element_type=f32)


def select3(x, weights, product):
    n = x.shape[0]
    y = product(terms3(x), weights)
    return y[:n] + y[n : 2 * n] + y[2 * n :]


def kernel(
    u_hbm,
    load_hbm,
    mass_hbm,
    offset_hbm,
    dofs_hbm,
    owner_hbm,
    basis_hbm,
    stiff_hbm,
    k_hbm,
    s_hbm,
    out,
    u_v,
    load_v,
    mass_v,
    offset_v,
    dofs_v,
    owner_v,
    basis_v,
    stiff_v,
    table_v,
    near_hi,
    near_lo,
    far_hi,
    far_lo,
    perm,
    slots,
    slots_side,
    send1,
    recv1,
    send2,
    recv2,
    sendp,
    recvp,
    travel_v,
    total_v,
    sendg,
    recvg,
    recvg_side,
    fixed,
    fixed_side,
    base_v,
    base_side,
    u_side,
    local_sem,
    send_sem,
    recv_sem,
    side_send,
    side_recv,
    ready,
):
    g = lax.axis_index("grp")
    h = lax.axis_index("harm")
    chip = lax.div(h, 2)
    core = lax.rem(h, 2)
    sides = (lax.rem(g + 1, GRP), lax.rem(g + GRP - 1, GRP))

    far = [(4 * (chip ^ (g >> 2) ^ 4) + t, 2 * chip + 1 - core) for t in range(4)]

    def place(part):
        y = part >> 1
        return 2 * jnp.where(y < 4, y, 11 - y) + (part & 1)

    def far_place(group, part):
        return 8 * (group & 7) + 2 * (group >> 3) + (part & 1)

    mates = [lax.rem(h + k, PARTS) for k in (8, 7, 9, 6, 10, 5, 11, 4, 12, 3, 13, 2, 14, 1, 15)]
    exists = (g < GRP - 1, g > 0)
    later_side = [there & ((side & 7) > (g & 7)) for there, side in zip(exists, sides)]
    earlier_side = [there & ((side & 7) < (g & 7)) for there, side in zip(exists, sides)]
    later_far = [far_place(*peer) > far_place(g, h) for peer in far]
    n_mates = PARTS - 1 - place(h)
    n_sides = sum(later.astype(i32) for later in later_side)
    n_before = sum(earlier.astype(i32) for earlier in earlier_side)
    n_far = sum(later.astype(i32) for later in later_far)
    barrier = pltpu.get_barrier_semaphore()

    def signal(sem, group, part):
        pl.semaphore_signal(sem, inc=1, device_id=(group, part), device_id_type=MESH)

    def tell(later, sems):
        def when(flag, peers, sem):
            @pl.when(flag)
            def _():
                for group, part in peers:
                    signal(sem, group, part)

        side_flags = later_side if later else earlier_side
        for flag, peer in zip(later_far, far):
            when(flag if later else jnp.logical_not(flag), [peer], sems[2])
        for d, side in enumerate(sides):
            when(side_flags[d], [(side, h)], sems[5 - d])

        def mate(p, _):
            y = p >> 1
            signal(sems[0], g, 2 * jnp.where(y < 4, y, 11 - y) + (p & 1))
            return 0

        mine = place(h)
        lax.fori_loop(mine + 1 if later else 0, PARTS if later else mine, mate, 0)
        for d, side in enumerate(sides):
            others = [(side, 2 * lax.rem(chip + k, CHIPS) + core) for k in (4, 3, 5, 2, 6, 1, 7)]
            when(side_flags[d], others, sems[3])

    tell(True, [barrier] * 6)

    def await_some(sem, n):
        @pl.when(n > 0)
        def _():
            pl.semaphore_wait(sem, n)

    await_some(barrier, (PARTS - 1 - n_mates) + CHIPS * n_before + (4 - n_far))
    def side_copies(n, src, dst):
        return [
            pltpu.make_async_remote_copy(
                src_ref=src.at[:, 256:512] if k == 0 else src.at[:, 0:256],
                dst_ref=dst.at[k],
                send_sem=side_send.at[n, k],
                recv_sem=side_recv.at[n, k],
                device_id=(side, h),
                device_id_type=MESH,
            )
            for k, side in enumerate(sides)
        ]

    def start_if(copies, flags):
        for copy, flag in zip(copies, flags):
            pl.when(flag)(copy.start)

    halo0 = side_copies(0, u_hbm, u_side)
    start_if(halo0, earlier_side)

    tell(False, [ready.at[i] for i in range(6)])

    fetches = [
        pltpu.make_async_copy(src, dst, local_sem.at[i])
        for i, (src, dst) in enumerate(
            [
                (owner_hbm, owner_v),
                (dofs_hbm, dofs_v),
                (u_hbm, u_v),
                (load_hbm, load_v),
                (mass_hbm, mass_v),
                (offset_hbm, offset_v),
                (k_hbm, table_v.at[0]),
                (s_hbm, table_v.at[1]),
                (stiff_hbm, stiff_v),
                (basis_hbm, basis_v),
            ]
        )
    ]
    for fetch in fetches:
        fetch.start()

    def wait_sides(copies):
        for copy, there in zip(copies, (g > 0, g < GRP - 1)):
            pl.when(there)(copy.wait_recv)

    for k, there in enumerate((g > 0, g < GRP - 1)):

        @pl.when(jnp.logical_not(there))
        def _():
            for ref in (u_side, fixed_side, base_side, recvg_side):
                ref[k] = jnp.zeros(ref.shape[1:], f32)

    def send_sides(n, src, dst):
        copies = side_copies(n, src, dst)
        start_if(copies, exists)
        return copies

    def send_parts(n, src, dst):
        for to in mates:
            pltpu.make_async_remote_copy(
                src_ref=src.at[lax.div(to, 2)],
                dst_ref=dst.at[h],
                send_sem=send_sem.at[n],
                recv_sem=recv_sem.at[n],
                device_id=(g, to),
                device_id_type=MESH,
            ).start()
        dst[h] = src[chip]

    def settle(ref, sem):
        pltpu.make_async_copy(ref, ref, sem).wait()

    def settle_sides(sems, flags):
        for d, there in enumerate(flags):

            @pl.when(there)
            def _():
                settle(recvg_side.at[d], sems.at[5 + d])

    fetches[0].wait()
    fetches[1].wait()
    owner = owner_v[...]
    own = jnp.where(lax.broadcasted_iota(i32, (GRP, JOINTS), 0) == owner, 1.0, 0.0)
    before = jnp.where(
        lax.broadcasted_iota(i32, (JOINTS, JOINTS), 0)
        < lax.broadcasted_iota(i32, (JOINTS, JOINTS), 1),
        1.0,
        0.0,
    )
    earlier = mm(own.astype(bf16), before.astype(bf16))
    rank = jnp.sum(earlier * own, axis=0, keepdims=True)
    tile = ((owner >> 2) ^ (g >> 2) ^ 4).astype(f32)
    lane = ((owner & 3) * CAP).astype(f32) + rank
    ones = jnp.ones((1, JOINTS), f32)
    dofs = dofs_v[...]
    row = lax.broadcasted_iota(i32, (128, DOF), 0)
    for m in range(DOF // 128):
        perm[m * 128 : (m + 1) * 128, :] = jnp.where(row == dofs - m * 128, 1.0, 0.0).astype(bf16)
    by_joint = jnp.concatenate(
        [
            jnp.concatenate([tile, lane, ones], axis=0),
            jnp.concatenate([tile, lane, -ones], axis=0),
        ],
        axis=1,
    )
    by_dof = mm_t(by_joint.astype(bf16), perm[...])
    slot_f = by_dof[0:1] * 128.0 + by_dof[1:2]
    slot = slot_f.astype(i32)
    sign = by_dof[2:3]
    for m in range(CHIPS):
        slots[m * 128 : (m + 1) * 128, :] = jnp.where(row == slot - m * 128, 1.0, 0.0).astype(bf16)

    fetches[2].wait()
    u0 = u_v[...]

    def to_slots(x, out):
        by_slot = select3(x, slots[...], mm_t)
        for m in range(CHIPS):
            for n in range(x.shape[0] // CD):
                out[m, n] = by_slot[n * CD : (n + 1) * CD, m * 128 : (m + 1) * 128]

    fetches[6].wait()
    fetches[7].wait()
    at = lax.broadcasted_iota(i32, (8, 128), 1)
    quarters = [(at >= q * CAP) & (at < (q + 1) * CAP) for q in range(4)]
    for t in range(4):
        column = far[t][0] * CAP
        begin = jnp.minimum(lax.div(column, 128), 4)
        packed = jnp.zeros((8, 128), f32)
        for q in range(4):
            rows = pl.ds(8 * (q % 2), 8)
            part = table_v[q // 2, 0, rows, pl.ds(pl.multiple_of(begin * 128, 128), 256)]
            shift = lax.rem(q * CAP - (column - begin * 128) + 512, 256)
            packed = jnp.where(quarters[q], pltpu.roll(part, shift, 1)[:, :128], packed)
        sendp[t] = packed
    tables = [
        pltpu.make_async_remote_copy(
            src_ref=sendp.at[t],
            dst_ref=recvp.at[lax.rem(g, 4)],
            send_sem=send_sem.at[2],
            recv_sem=recv_sem.at[2],
            device_id=peer,
            device_id_type=MESH,
        )
        for t, peer in enumerate(far)
    ]
    start_if(tables, [jnp.logical_not(later) for later in later_far])

    fetches[8].wait()
    eye = lax.broadcasted_iota(i32, (128, 128), 0) == lax.broadcasted_iota(i32, (128, 128), 1)
    diagonals = []

    def store(hi, lo, i, at, block):
        high, low = split2(block)
        hi[i, :, at : at + 128] = high.astype(bf16)
        lo[i, :, at : at + 128] = low.astype(bf16)

    for i in range(4):
        own_block = stiff_v[i, 0]
        diagonals.append(jnp.sum(jnp.where(eye, own_block, 0.0), axis=0, keepdims=True))
        store(near_hi, near_lo, i, 0, jnp.where(eye, 0.0, own_block))
        store(near_hi, near_lo, i, 128, stiff_v[i, 2 if i < 2 else 1])
        store(far_hi, far_lo, i, 0, stiff_v[i, 1 if i < 2 else 2])
    kdiag = jnp.concatenate(diagonals, axis=1)
    coef = 4 * h + lax.broadcasted_iota(i32, (CD, DOF), 0)
    freq = jnp.where(coef <= HARM, coef, coef - HARM).astype(f32) * (1.0 / HARM)
    fetches[4].wait()
    net = kdiag - (freq * freq) * mass_v[...]
    precond = 1.0 / net
    signed = precond * sign
    to_slots(jnp.concatenate([u0 * sign, precond], axis=0), send1)
    fixed[...] = jnp.concatenate([signed, jnp.broadcast_to(slot_f, (CD, DOF))], axis=0)
    fetches[5].wait()
    offset = offset_v[...]

    def block(u, i):
        return u[:, i * 128 : (i + 1) * 128]

    def nearer(i, k):
        return jnp.abs(offset[k : k + 1, i : i + 1]) == 1

    def apply(lhs, hi, lo):
        terms = terms2(lhs)
        a = mm_t(terms, hi)
        b = mm_t(terms, lo)
        return a[:CD] + (a[CD:] + b[:CD])

    def near_product(u):
        parts = []
        for i in range(4):
            if i < 2:
                other = jnp.where(nearer(i, 1), block(u, i + 1), block(u, i + 2))
            else:
                other = jnp.where(nearer(i, 0), block(u, i - 1), block(u, i - 2))
            lhs = jnp.concatenate([block(u, i), other], axis=1)
            parts.append(apply(lhs, near_hi[i], near_lo[i]))
        return jnp.concatenate(parts, axis=1)

    def far_product(u, low, high):
        others = [
            jnp.where(nearer(0, 0), block(low, 1), block(low, 0)),
            jnp.where(nearer(1, 0), block(u, 0), block(low, 1)),
            jnp.where(nearer(2, 1), block(u, 3), block(high, 0)),
            jnp.where(nearer(3, 1), block(high, 0), block(high, 1)),
        ]
        return jnp.concatenate(
            [apply(others[i], far_hi[i], far_lo[i]) for i in range(4)], axis=1
        )

    fetches[3].wait()
    load = load_v[...]
    part = load - near_product(u0)
    def halo_later(d):
        @pl.when(later_side[d])
        def _():
            pl.semaphore_wait(ready.at[4 + d], 1)
            halo0[d].start()

    halo_later(0)
    await_some(ready.at[0], n_mates)
    send_parts(0, send1, recv1)
    halo_later(1)
    halof = send_sides(1, fixed, fixed_side)
    def tables_later(now):
        await_some(ready.at[2], jnp.where(now, n_far, 0))
        start_if(tables, [now & later for later in later_far])

    tables_later((g & 7) > 0)


    wait_sides(halo0)
    base = precond * (part - far_product(u0, u_side[0], u_side[1]))
    to_slots(base * sign, send2)
    send_parts(1, send2, recv2)
    tables_later((g & 7) == 0)
    base_v[...] = base
    halob = send_sides(2, base_v, base_side)

    fetches[9].wait()
    settle(recv1.at[pl.ds(0, PARTS - 1)], recv_sem.at[0])
    settle(recvp, recv_sem.at[2])
    table = []
    for r in range(4):
        rows = jnp.zeros((8, 128), f32)
        for q in range(4):
            part = recvp[q]
            if q != r:
                part = pltpu.roll(part, ((q - r) * CAP) % 128, 1)
            rows = jnp.where(quarters[q], part, rows)
        table.append(rows)
    k_slot = jnp.concatenate(table[:2], axis=0)
    s_slot = jnp.concatenate(table[2:], axis=0)
    minus_s = -s_slot

    def forces(x, n):
        high, low = split2(x.reshape(2 * HARM, 128))
        high, low = high.astype(bf16), low.astype(bf16)
        high_t, low_t = basis_v[0, :, : 2 * HARM], basis_v[1, :, : 2 * HARM]
        travel_v[...] = mm(high_t, high) + (mm(low_t, high) + mm(high_t, low))

        def samples(i, p):
            at = pl.multiple_of(8 * i, 8)
            travel = travel_v[pl.ds(at, 8), :]
            sums = []
            for j in range(8):
                m = k_slot * travel[j : j + 1, :]
                p = jnp.minimum(jnp.maximum(p, minus_s - m), s_slot - m)
                sums.append(jnp.sum(p + m, axis=0, keepdims=True))
            total_v[pl.ds(at, 8), :] = jnp.concatenate(sums, axis=0)
            return p

        lax.fori_loop(0, NT // 8, samples, jnp.zeros((NE, 128), f32), unroll=4)
        high, low = split2(total_v[...])
        high, low = high.astype(bf16), low.astype(bf16)
        high_t, low_t = basis_v[2, : 2 * HARM], basis_v[3, : 2 * HARM]
        coefs = mm(high_t, high) + (mm(low_t, high) + mm(high_t, low))
        sendg[n] = coefs.reshape(PARTS, CD, 128)
        if n == 0:
            await_some(ready.at[3], (CHIPS - 1) * n_sides)
        for k in (4, 3, 5, 2, 6, 1, 7, 0):
            to = 2 * lax.rem(chip + k, CHIPS) + core
            if n == 0:
                copies = [
                    pltpu.make_async_remote_copy(
                        src_ref=sendg.at[0, to],
                        dst_ref=recvg_side.at[d, chip],
                        send_sem=send_sem.at[5 + d],
                        recv_sem=recv_sem.at[5 + d],
                        device_id=(side, to),
                        device_id_type=MESH,
                    )
                    for d, side in enumerate(sides)
                ]
                start_if(copies, exists)
            if k > 0:
                pltpu.make_async_remote_copy(
                    src_ref=sendg.at[n, to],
                    dst_ref=recvg.at[n, chip],
                    send_sem=send_sem.at[3 + n],
                    recv_sem=recv_sem.at[3 + n],
                    device_id=(g, to),
                    device_id_type=MESH,
                ).start()
        recvg[n, chip] = sendg[n, h]

    def to_dofs(x, weights):
        lanes = jnp.concatenate([x[m] for m in range(CHIPS)], axis=1)
        return select3(lanes, weights, mm)

    forces(recv1[:, 0], 0)
    settle(recv2.at[pl.ds(0, PARTS - 1)], recv_sem.at[1])
    forces(recv2[:, 0] - recv1[:, 1] * sendg[0], 1)

    wait_sides(halof)
    row = lax.broadcasted_iota(i32, (128, DOF // 2), 0)
    for k in range(2):
        slot_side = fixed_side[k, CD : CD + 1, :].astype(i32)
        for m in range(CHIPS):
            slots_side[k, m * 128 : (m + 1) * 128, :] = jnp.where(
                row == slot_side - m * 128, 1.0, 0.0
            ).astype(bf16)

    settle(recvg.at[0, pl.ds(0, CHIPS - 1)], recv_sem.at[3])
    u1 = base - signed * to_dofs(recvg[0], slots[...])
    part = near_product(u1) + net * u1 - load
    wait_sides(halob)
    settle(recvg.at[1, pl.ds(0, CHIPS - 1)], recv_sem.at[4])
    part = part + sign * to_dofs(recvg[1], slots[...])
    settle_sides(recv_sem, (g > 0, g < GRP - 1))
    low, high = [
        base_side[k] - fixed_side[k, :CD, :] * to_dofs(recvg_side[k], slots_side[k])
        for k in range(2)
    ]
    residual = part + far_product(u1, low, high)
    out[1] = residual
    out[0] = u1 - precond * residual

    for copies in (halo0, halof, halob):
        for copy, there in zip(copies, exists):
            pl.when(there)(copy.wait_send)
    settle(recv1.at[pl.ds(0, PARTS - 1)], send_sem.at[0])
    settle(recv2.at[pl.ds(0, PARTS - 1)], send_sem.at[1])
    settle(recvp, send_sem.at[2])
    for n in range(2):
        settle(recvg.at[n, pl.ds(0, CHIPS - 1)], send_sem.at[3 + n])
    settle_sides(send_sem, exists)


def local(u, load, mass, stiffness, offset, dofs, owner, k_table, s_table):
    basis = jnp.asarray(basis_tables())
    hbm = pl.BlockSpec(memory_space=pltpu.HBM)
    vmem = pl.BlockSpec(memory_space=pltpu.VMEM)
    out = pl.pallas_call(
        kernel,
        out_shape=pltpu.VMEM((2, CD, DOF), f32),
        in_specs=[hbm] * 10,
        out_specs=vmem,
        scratch_shapes=[
            pltpu.VMEM((CD, DOF), f32),
            pltpu.VMEM((CD, DOF), f32),
            pltpu.VMEM((1, DOF), f32),
            pltpu.VMEM((2, 4), i32),
            pltpu.VMEM((1, DOF), i32),
            pltpu.VMEM((1, JOINTS), i32),
            pltpu.VMEM((4, 128, 128), bf16),
            pltpu.VMEM((4, 3, 128, 128), f32),
            pltpu.VMEM((2, 1, NE, GRP * CAP), f32),
            pltpu.VMEM((4, 128, 256), bf16),
            pltpu.VMEM((4, 128, 256), bf16),
            pltpu.VMEM((4, 128, 128), bf16),
            pltpu.VMEM((4, 128, 128), bf16),
            pltpu.VMEM((DOF, DOF), bf16),
            pltpu.VMEM((CHIPS * 128, DOF), bf16),
            pltpu.VMEM((2, CHIPS * 128, DOF // 2), bf16),
            pltpu.VMEM((CHIPS, 2, CD, 128), f32),
            pltpu.VMEM((PARTS, 2, CD, 128), f32),
            pltpu.VMEM((CHIPS, 1, CD, 128), f32),
            pltpu.VMEM((PARTS, 1, CD, 128), f32),
            pltpu.VMEM((4, 8, 128), f32),
            pltpu.VMEM((4, 8, 128), f32),
            pltpu.VMEM((NT, 128), f32),
            pltpu.VMEM((NT, 128), f32),
            pltpu.VMEM((2, PARTS, CD, 128), f32),
            pltpu.VMEM((2, CHIPS, CD, 128), f32),
            pltpu.VMEM((2, CHIPS, CD, 128), f32),
            pltpu.VMEM((8, DOF), f32),
            pltpu.VMEM((2, 8, DOF // 2), f32),
            pltpu.VMEM((CD, DOF), f32),
            pltpu.VMEM((2, CD, DOF // 2), f32),
            pltpu.VMEM((2, CD, DOF // 2), f32),
            pltpu.SemaphoreType.DMA((10,)),
            pltpu.SemaphoreType.DMA((7,)),
            pltpu.SemaphoreType.DMA((7,)),
            pltpu.SemaphoreType.DMA((3, 2)),
            pltpu.SemaphoreType.DMA((3, 2)),
            pltpu.SemaphoreType.REGULAR((6,)),
        ],
        compiler_params=pltpu.CompilerParams(
            collective_id=0, has_side_effects=True, vmem_limit_bytes=60 * 2**20
        ),
    )(u, load, mass.reshape(1, DOF), offset.T, dofs, owner, basis, stiffness, k_table, s_table)
    return out[0], out[1]


def solution(mesh):
    in_specs = (
        P("harm", "grp"),
        P("harm", "grp"),
        P("grp"),
        P("grp", None, None, None),
        P("grp", None),
        P("grp", None),
        P("grp", None),
        P("grp", None, None),
        P("grp", None, None),
    )
    out_specs = (P("harm", "grp"), P("harm", "grp"))

    def run(*args):
        return tuple(local(*args))

    return jax.shard_map(run, mesh=mesh, in_specs=in_specs, out_specs=out_specs, check_vma=False)
```

```python
import math

import jax
import jax.numpy as jnp
import numpy as np
from jax import lax
from jax.experimental import pallas as pl
from jax.experimental.pallas import tpu as pltpu
from jax.sharding import PartitionSpec as P

HARM = 32
NT = 128
GRP = 32
PARTS = 16
CHIPS = 8
CD = 4
DOF = 512
JOINTS = 256
CAP = 24
NE = 16
f32, bf16, i32 = jnp.float32, jnp.bfloat16, jnp.int32
MESH = pl.DeviceIdType.MESH


def basis_tables():
    coef = np.arange(2 * HARM)
    harmonic = np.where(coef <= HARM, coef, coef - HARM)
    angle = 2.0 * math.pi * ((np.arange(NT)[:, None] * harmonic[None, :]) % NT) / NT
    synth = np.where(coef > HARM, np.sin(angle), np.cos(angle))
    travel = np.zeros((NT, NT), np.float32)
    travel[:, : 2 * HARM] = synth - synth[-1:]
    project = np.zeros((NT, NT), np.float32)
    project[: 2 * HARM] = (synth * np.where(coef == 0, 1.0, 2.0) / NT).T

    def split(x):
        high = x.astype(jnp.bfloat16)
        return [high, (x - high.astype(np.float32)).astype(jnp.bfloat16)]

    return np.stack(split(travel) + split(project))


def split2(x):
    high = x.astype(bf16).astype(f32)
    return high, x - high


def terms2(x):
    return jnp.concatenate(split2(x), axis=0).astype(bf16)


def mm(a, b):
    return lax.dot_general(a, b, (((1,), (0,)), ((), ())), preferred_element_type=f32)


def mm_t(a, b):
    return lax.dot_general(a, b, (((1,), (1,)), ((), ())), preferred_element_type=f32)


def select2(x, weights, product):
    n = x.shape[0]
    y = product(terms2(x), weights)
    return y[:n] + y[n:]


def kernel(
    u_hbm,
    load_hbm,
    mass_hbm,
    offset_hbm,
    dofs_hbm,
    owner_hbm,
    basis_hbm,
    stiff_hbm,
    k_hbm,
    s_hbm,
    out,
    u_v,
    load_v,
    mass_v,
    offset_v,
    dofs_v,
    owner_v,
    basis_v,
    stiff_v,
    table_v,
    near_hi,
    near_lo,
    far_hi,
    far_lo,
    perm,
    slots,
    slots_side,
    send1,
    recv1,
    send2,
    recv2,
    sendp,
    recvp,
    travel_v,
    total_v,
    sendg,
    recvg,
    recvg_side,
    fixed,
    fixed_side,
    base_v,
    base_side,
    u_side,
    local_sem,
    send_sem,
    recv_sem,
    side_send,
    side_recv,
    ready,
):
    g = lax.axis_index("grp")
    h = lax.axis_index("harm")
    chip = lax.div(h, 2)
    core = lax.rem(h, 2)
    sides = (lax.rem(g + 1, GRP), lax.rem(g + GRP - 1, GRP))

    far = [(4 * (chip ^ (g >> 2) ^ 4) + t, 2 * chip + 1 - core) for t in range(4)]

    def place(part):
        y = part >> 1
        return 2 * jnp.where(y < 4, y, 11 - y) + (part & 1)

    def far_place(group, part):
        return 8 * (group & 7) + 2 * (group >> 3) + (part & 1)

    mates = [lax.rem(h + k, PARTS) for k in (8, 7, 9, 6, 10, 5, 11, 4, 12, 3, 13, 2, 14, 1, 15)]
    exists = (g < GRP - 1, g > 0)
    later_side = [there & ((side & 7) > (g & 7)) for there, side in zip(exists, sides)]
    earlier_side = [there & ((side & 7) < (g & 7)) for there, side in zip(exists, sides)]
    later_far = [far_place(*peer) > far_place(g, h) for peer in far]
    n_mates = PARTS - 1 - place(h)
    n_sides = sum(later.astype(i32) for later in later_side)
    n_before = sum(earlier.astype(i32) for earlier in earlier_side)
    n_far = sum(later.astype(i32) for later in later_far)
    barrier = pltpu.get_barrier_semaphore()

    def signal(sem, group, part):
        pl.semaphore_signal(sem, inc=1, device_id=(group, part), device_id_type=MESH)

    def tell(later, sems):
        def when(flag, peers, sem):
            @pl.when(flag)
            def _():
                for group, part in peers:
                    signal(sem, group, part)

        side_flags = later_side if later else earlier_side
        for flag, peer in zip(later_far, far):
            when(flag if later else jnp.logical_not(flag), [peer], sems[2])
        for d, side in enumerate(sides):
            when(side_flags[d], [(side, h)], sems[5 - d])

        def mate(p, _):
            y = p >> 1
            signal(sems[0], g, 2 * jnp.where(y < 4, y, 11 - y) + (p & 1))
            return 0

        mine = place(h)
        lax.fori_loop(mine + 1 if later else 0, PARTS if later else mine, mate, 0)
        for d, side in enumerate(sides):
            others = [(side, 2 * lax.rem(chip + k, CHIPS) + core) for k in (4, 3, 5, 2, 6, 1, 7)]
            when(side_flags[d], others, sems[3])

    tell(True, [barrier] * 6)

    def await_some(sem, n):
        @pl.when(n > 0)
        def _():
            pl.semaphore_wait(sem, n)

    await_some(barrier, (PARTS - 1 - n_mates) + CHIPS * n_before + (4 - n_far))
    def side_copies(n, src, dst):
        return [
            pltpu.make_async_remote_copy(
                src_ref=src.at[:, 256:512] if k == 0 else src.at[:, 0:256],
                dst_ref=dst.at[k],
                send_sem=side_send.at[n, k],
                recv_sem=side_recv.at[n, k],
                device_id=(side, h),
                device_id_type=MESH,
            )
            for k, side in enumerate(sides)
        ]

    def start_if(copies, flags):
        for copy, flag in zip(copies, flags):
            pl.when(flag)(copy.start)

    halo0 = side_copies(0, u_hbm, u_side)
    start_if(halo0, earlier_side)

    tell(False, [ready.at[i] for i in range(6)])

    fetches = [
        pltpu.make_async_copy(src, dst, local_sem.at[i])
        for i, (src, dst) in enumerate(
            [
                (owner_hbm, owner_v),
                (dofs_hbm, dofs_v),
                (u_hbm, u_v),
                (load_hbm, load_v),
                (mass_hbm, mass_v),
                (offset_hbm, offset_v),
                (k_hbm, table_v.at[0]),
                (s_hbm, table_v.at[1]),
                (stiff_hbm, stiff_v),
                (basis_hbm, basis_v),
            ]
        )
    ]
    for fetch in fetches:
        fetch.start()

    def wait_sides(copies):
        for copy, there in zip(copies, (g > 0, g < GRP - 1)):
            pl.when(there)(copy.wait_recv)

    for k, there in enumerate((g > 0, g < GRP - 1)):

        @pl.when(jnp.logical_not(there))
        def _():
            for ref in (u_side, fixed_side, base_side, recvg_side):
                ref[k] = jnp.zeros(ref.shape[1:], f32)

    def send_sides(n, src, dst):
        copies = side_copies(n, src, dst)
        start_if(copies, exists)
        return copies

    def send_parts(n, src, dst):
        for to in mates:
            pltpu.make_async_remote_copy(
                src_ref=src.at[lax.div(to, 2)],
                dst_ref=dst.at[h],
                send_sem=send_sem.at[n],
                recv_sem=recv_sem.at[n],
                device_id=(g, to),
                device_id_type=MESH,
            ).start()
        dst[h] = src[chip]

    def settle(ref, sem):
        pltpu.make_async_copy(ref, ref, sem).wait()

    def settle_sides(sems, flags):
        for d, there in enumerate(flags):

            @pl.when(there)
            def _():
                settle(recvg_side.at[d], sems.at[5 + d])

    fetches[0].wait()
    fetches[1].wait()
    owner = owner_v[...]
    own = jnp.where(lax.broadcasted_iota(i32, (GRP, JOINTS), 0) == owner, 1.0, 0.0)
    before = jnp.where(
        lax.broadcasted_iota(i32, (JOINTS, JOINTS), 0)
        < lax.broadcasted_iota(i32, (JOINTS, JOINTS), 1),
        1.0,
        0.0,
    )
    earlier = mm(own.astype(bf16), before.astype(bf16))
    rank = jnp.sum(earlier * own, axis=0, keepdims=True)
    tile = ((owner >> 2) ^ (g >> 2) ^ 4).astype(f32)
    lane = ((owner & 3) * CAP).astype(f32) + rank
    ones = jnp.ones((1, JOINTS), f32)
    dofs = dofs_v[...]
    row = lax.broadcasted_iota(i32, (128, DOF), 0)
    for m in range(DOF // 128):
        perm[m * 128 : (m + 1) * 128, :] = jnp.where(row == dofs - m * 128, 1.0, 0.0).astype(bf16)
    by_joint = jnp.concatenate(
        [
            jnp.concatenate([tile, lane, ones], axis=0),
            jnp.concatenate([tile, lane, -ones], axis=0),
        ],
        axis=1,
    )
    by_dof = mm_t(by_joint.astype(bf16), perm[...])
    slot_f = by_dof[0:1] * 128.0 + by_dof[1:2]
    slot = slot_f.astype(i32)
    sign = by_dof[2:3]
    for m in range(CHIPS):
        slots[m * 128 : (m + 1) * 128, :] = jnp.where(row == slot - m * 128, 1.0, 0.0).astype(bf16)

    fetches[2].wait()
    u0 = u_v[...]

    def to_slots(x, out):
        by_slot = select2(x, slots[...], mm_t)
        for m in range(CHIPS):
            for n in range(x.shape[0] // CD):
                out[m, n] = by_slot[n * CD : (n + 1) * CD, m * 128 : (m + 1) * 128]

    fetches[6].wait()
    fetches[7].wait()
    at = lax.broadcasted_iota(i32, (8, 128), 1)
    quarters = [(at >= q * CAP) & (at < (q + 1) * CAP) for q in range(4)]
    for t in range(4):
        column = far[t][0] * CAP
        begin = jnp.minimum(lax.div(column, 128), 4)
        packed = jnp.zeros((8, 128), f32)
        for q in range(4):
            rows = pl.ds(8 * (q % 2), 8)
            part = table_v[q // 2, 0, rows, pl.ds(pl.multiple_of(begin * 128, 128), 256)]
            shift = lax.rem(q * CAP - (column - begin * 128) + 512, 256)
            packed = jnp.where(quarters[q], pltpu.roll(part, shift, 1)[:, :128], packed)
        sendp[t] = packed
    tables = [
        pltpu.make_async_remote_copy(
            src_ref=sendp.at[t],
            dst_ref=recvp.at[lax.rem(g, 4)],
            send_sem=send_sem.at[2],
            recv_sem=recv_sem.at[2],
            device_id=peer,
            device_id_type=MESH,
        )
        for t, peer in enumerate(far)
    ]
    start_if(tables, [jnp.logical_not(later) for later in later_far])

    fetches[8].wait()
    eye = lax.broadcasted_iota(i32, (128, 128), 0) == lax.broadcasted_iota(i32, (128, 128), 1)
    diagonals = []

    def store(hi, lo, i, at, block):
        high, low = split2(block)
        hi[i, :, at : at + 128] = high.astype(bf16)
        lo[i, :, at : at + 128] = low.astype(bf16)

    for i in range(4):
        own_block = stiff_v[i, 0]
        diagonals.append(jnp.sum(jnp.where(eye, own_block, 0.0), axis=0, keepdims=True))
        store(near_hi, near_lo, i, 0, jnp.where(eye, 0.0, own_block))
        store(near_hi, near_lo, i, 128, stiff_v[i, 2 if i < 2 else 1])
        store(far_hi, far_lo, i, 0, stiff_v[i, 1 if i < 2 else 2])
    kdiag = jnp.concatenate(diagonals, axis=1)
    coef = 4 * h + lax.broadcasted_iota(i32, (CD, DOF), 0)
    freq = jnp.where(coef <= HARM, coef, coef - HARM).astype(f32) * (1.0 / HARM)
    fetches[4].wait()
    net = kdiag - (freq * freq) * mass_v[...]
    precond = 1.0 / net
    signed = precond * sign
    to_slots(jnp.concatenate([u0 * sign, precond], axis=0), send1)
    fixed[...] = jnp.concatenate([signed, jnp.broadcast_to(slot_f, (CD, DOF))], axis=0)
    fetches[5].wait()
    offset = offset_v[...]

    def block(u, i):
        return u[:, i * 128 : (i + 1) * 128]

    def nearer(i, k):
        return jnp.abs(offset[k : k + 1, i : i + 1]) == 1

    def apply(lhs, hi, lo):
        terms = terms2(lhs)
        a = mm_t(terms, hi)
        b = mm_t(terms, lo)
        return a[:CD] + (a[CD:] + b[:CD])

    def near_product(u):
        parts = []
        for i in range(4):
            if i < 2:
                other = jnp.where(nearer(i, 1), block(u, i + 1), block(u, i + 2))
            else:
                other = jnp.where(nearer(i, 0), block(u, i - 1), block(u, i - 2))
            lhs = jnp.concatenate([block(u, i), other], axis=1)
            parts.append(apply(lhs, near_hi[i], near_lo[i]))
        return jnp.concatenate(parts, axis=1)

    def far_product(u, low, high):
        others = [
            jnp.where(nearer(0, 0), block(low, 1), block(low, 0)),
            jnp.where(nearer(1, 0), block(u, 0), block(low, 1)),
            jnp.where(nearer(2, 1), block(u, 3), block(high, 0)),
            jnp.where(nearer(3, 1), block(high, 0), block(high, 1)),
        ]
        return jnp.concatenate(
            [apply(others[i], far_hi[i], far_lo[i]) for i in range(4)], axis=1
        )

    fetches[3].wait()
    load = load_v[...]
    part = load - near_product(u0)
    def halo_later(d):
        @pl.when(later_side[d])
        def _():
            pl.semaphore_wait(ready.at[4 + d], 1)
            halo0[d].start()

    halo_later(0)
    await_some(ready.at[0], n_mates)
    send_parts(0, send1, recv1)
    halo_later(1)
    halof = send_sides(1, fixed, fixed_side)
    def tables_later(now):
        await_some(ready.at[2], jnp.where(now, n_far, 0))
        start_if(tables, [now & later for later in later_far])

    tables_later((g & 7) > 0)


    wait_sides(halo0)
    base = precond * (part - far_product(u0, u_side[0], u_side[1]))
    to_slots(base * sign, send2)
    send_parts(1, send2, recv2)
    tables_later((g & 7) == 0)
    base_v[...] = base
    halob = send_sides(2, base_v, base_side)

    fetches[9].wait()
    settle(recv1.at[pl.ds(0, PARTS - 1)], recv_sem.at[0])
    settle(recvp, recv_sem.at[2])
    table = []
    for r in range(4):
        rows = jnp.zeros((8, 128), f32)
        for q in range(4):
            part = recvp[q]
            if q != r:
                part = pltpu.roll(part, ((q - r) * CAP) % 128, 1)
            rows = jnp.where(quarters[q], part, rows)
        table.append(rows)
    k_slot = jnp.concatenate(table[:2], axis=0)
    s_slot = jnp.concatenate(table[2:], axis=0)
    minus_s = -s_slot

    def forces(x, n):
        high, low = split2(x.reshape(2 * HARM, 128))
        high, low = high.astype(bf16), low.astype(bf16)
        high_t, low_t = basis_v[0, :, : 2 * HARM], basis_v[1, :, : 2 * HARM]
        travel_v[...] = mm(high_t, high) + (mm(low_t, high) + mm(high_t, low))

        def samples(i, p):
            at = pl.multiple_of(8 * i, 8)
            travel = travel_v[pl.ds(at, 8), :]
            sums = []
            for j in range(8):
                m = k_slot * travel[j : j + 1, :]
                p = jnp.minimum(jnp.maximum(p, minus_s - m), s_slot - m)
                sums.append(jnp.sum(p + m, axis=0, keepdims=True))
            total_v[pl.ds(at, 8), :] = jnp.concatenate(sums, axis=0)
            return p

        lax.fori_loop(0, NT // 8, samples, jnp.zeros((NE, 128), f32), unroll=16)
        high, low = split2(total_v[...])
        high, low = high.astype(bf16), low.astype(bf16)
        high_t, low_t = basis_v[2, : 2 * HARM], basis_v[3, : 2 * HARM]
        coefs = mm(high_t, high) + (mm(low_t, high) + mm(high_t, low))
        sendg[n] = coefs.reshape(PARTS, CD, 128)
        if n == 0:
            await_some(ready.at[3], (CHIPS - 1) * n_sides)
        for k in (4, 3, 5, 2, 6, 1, 7, 0):
            to = 2 * lax.rem(chip + k, CHIPS) + core
            if n == 0:
                copies = [
                    pltpu.make_async_remote_copy(
                        src_ref=sendg.at[0, to],
                        dst_ref=recvg_side.at[d, chip],
                        send_sem=send_sem.at[5 + d],
                        recv_sem=recv_sem.at[5 + d],
                        device_id=(side, to),
                        device_id_type=MESH,
                    )
                    for d, side in enumerate(sides)
                ]
                start_if(copies, exists)
            if k > 0:
                pltpu.make_async_remote_copy(
                    src_ref=sendg.at[n, to],
                    dst_ref=recvg.at[n, chip],
                    send_sem=send_sem.at[3 + n],
                    recv_sem=recv_sem.at[3 + n],
                    device_id=(g, to),
                    device_id_type=MESH,
                ).start()
        recvg[n, chip] = sendg[n, h]

    def to_dofs(x, weights):
        lanes = jnp.concatenate([x[m] for m in range(CHIPS)], axis=1)
        return select2(lanes, weights, mm)

    forces(recv1[:, 0], 0)
    settle(recv2.at[pl.ds(0, PARTS - 1)], recv_sem.at[1])
    forces(recv2[:, 0] - recv1[:, 1] * sendg[0], 1)

    wait_sides(halof)
    row = lax.broadcasted_iota(i32, (128, DOF // 2), 0)
    for k in range(2):
        slot_side = fixed_side[k, CD : CD + 1, :].astype(i32)
        for m in range(CHIPS):
            slots_side[k, m * 128 : (m + 1) * 128, :] = jnp.where(
                row == slot_side - m * 128, 1.0, 0.0
            ).astype(bf16)

    settle(recvg.at[0, pl.ds(0, CHIPS - 1)], recv_sem.at[3])
    u1 = base - signed * to_dofs(recvg[0], slots[...])
    part = near_product(u1) + net * u1 - load
    wait_sides(halob)
    settle(recvg.at[1, pl.ds(0, CHIPS - 1)], recv_sem.at[4])
    part = part + sign * to_dofs(recvg[1], slots[...])
    settle_sides(recv_sem, (g > 0, g < GRP - 1))
    low, high = [
        base_side[k] - fixed_side[k, :CD, :] * to_dofs(recvg_side[k], slots_side[k])
        for k in range(2)
    ]
    residual = part + far_product(u1, low, high)
    out[1] = residual
    out[0] = u1 - precond * residual

    for copies in (halo0, halof, halob):
        for copy, there in zip(copies, exists):
            pl.when(there)(copy.wait_send)
    settle(recv1.at[pl.ds(0, PARTS - 1)], send_sem.at[0])
    settle(recv2.at[pl.ds(0, PARTS - 1)], send_sem.at[1])
    settle(recvp, send_sem.at[2])
    for n in range(2):
        settle(recvg.at[n, pl.ds(0, CHIPS - 1)], send_sem.at[3 + n])
    settle_sides(send_sem, exists)


def local(u, load, mass, stiffness, offset, dofs, owner, k_table, s_table):
    basis = jnp.asarray(basis_tables())
    hbm = pl.BlockSpec(memory_space=pltpu.HBM)
    vmem = pl.BlockSpec(memory_space=pltpu.VMEM)
    out = pl.pallas_call(
        kernel,
        out_shape=pltpu.VMEM((2, CD, DOF), f32),
        in_specs=[hbm] * 10,
        out_specs=vmem,
        scratch_shapes=[
            pltpu.VMEM((CD, DOF), f32),
            pltpu.VMEM((CD, DOF), f32),
            pltpu.VMEM((1, DOF), f32),
            pltpu.VMEM((2, 4), i32),
            pltpu.VMEM((1, DOF), i32),
            pltpu.VMEM((1, JOINTS), i32),
            pltpu.VMEM((4, 128, 128), bf16),
            pltpu.VMEM((4, 3, 128, 128), f32),
            pltpu.VMEM((2, 1, NE, GRP * CAP), f32),
            pltpu.VMEM((4, 128, 256), bf16),
            pltpu.VMEM((4, 128, 256), bf16),
            pltpu.VMEM((4, 128, 128), bf16),
            pltpu.VMEM((4, 128, 128), bf16),
            pltpu.VMEM((DOF, DOF), bf16),
            pltpu.VMEM((CHIPS * 128, DOF), bf16),
            pltpu.VMEM((2, CHIPS * 128, DOF // 2), bf16),
            pltpu.VMEM((CHIPS, 2, CD, 128), f32),
            pltpu.VMEM((PARTS, 2, CD, 128), f32),
            pltpu.VMEM((CHIPS, 1, CD, 128), f32),
            pltpu.VMEM((PARTS, 1, CD, 128), f32),
            pltpu.VMEM((4, 8, 128), f32),
            pltpu.VMEM((4, 8, 128), f32),
            pltpu.VMEM((NT, 128), f32),
            pltpu.VMEM((NT, 128), f32),
            pltpu.VMEM((2, PARTS, CD, 128), f32),
            pltpu.VMEM((2, CHIPS, CD, 128), f32),
            pltpu.VMEM((2, CHIPS, CD, 128), f32),
            pltpu.VMEM((8, DOF), f32),
            pltpu.VMEM((2, 8, DOF // 2), f32),
            pltpu.VMEM((CD, DOF), f32),
            pltpu.VMEM((2, CD, DOF // 2), f32),
            pltpu.VMEM((2, CD, DOF // 2), f32),
            pltpu.SemaphoreType.DMA((10,)),
            pltpu.SemaphoreType.DMA((7,)),
            pltpu.SemaphoreType.DMA((7,)),
            pltpu.SemaphoreType.DMA((3, 2)),
            pltpu.SemaphoreType.DMA((3, 2)),
            pltpu.SemaphoreType.REGULAR((6,)),
        ],
        compiler_params=pltpu.CompilerParams(
            collective_id=0, has_side_effects=True, vmem_limit_bytes=60 * 2**20
        ),
    )(u, load, mass.reshape(1, DOF), offset.T, dofs, owner, basis, stiffness, k_table, s_table)
    return out[0], out[1]


def solution(mesh):
    in_specs = (
        P("harm", "grp"),
        P("harm", "grp"),
        P("grp"),
        P("grp", None, None, None),
        P("grp", None),
        P("grp", None),
        P("grp", None),
        P("grp", None, None),
        P("grp", None, None),
    )
    out_specs = (P("harm", "grp"), P("harm", "grp"))

    def run(*args):
        return tuple(local(*args))

    return jax.shard_map(run, mesh=mesh, in_specs=in_specs, out_specs=out_specs, check_vma=False)
```
